128 devices in a mesh: ctx: 16 (over y, z), tp: 8 (over x, core).
Axes of the slice: x: 4, y: 4, z: 4, core: 2. Of those that a mesh axis runs over, the one named last changes fastest.
Arguments:
- queries: bfloat16 [16384, 4096], P('ctx', 'tp'), may hold values from -15 to 15
- keys: bfloat16 [16384, 256], P('ctx'), may hold values from -6 to 6
- values: bfloat16 [16384, 256], P('ctx'), may hold values from -6 to 6
- out_proj: bfloat16 [4096, 4096], P('tp', 'ctx'), may hold values from -0.09375 to 0.09375
- residual: bfloat16 [16384, 4096], P(('ctx', 'tp')), may hold values from -6 to 6
- norm_gain: float32 [4096], replicated, may hold values from 0.1 to 1.9
- expert_ids: int32 [16384, 4], P(('ctx', 'tp')), may hold values from 0 to 127, all different within a row; in each aligned block of 128 rows (0 to 127, 128 to 255, ...) at most 6 rows name the same one
- route_weights: float32 [16384, 4], P(('ctx', 'tp')), may hold values from 0.05 to 1
- w_in: bfloat16 [128, 4096, 1536], P(('ctx', 'tp')), may hold values from -0.09375 to 0.09375
- w_out: bfloat16 [128, 768, 4096], P(('ctx', 'tp')), may hold values from -0.21875 to 0.21875
Outputs:
- layer_out: bfloat16 [16384, 4096], P(('ctx', 'tp'))
The draws below stay inside these ranges and needn't reach their ends.
Inputs may be any that keep to these rules, and one draw needn't show every extreme that they name: `expert_ids`: each token names 4 different experts. Among the 128 tokens of one device (aligned blocks of rows) no expert is named by more than 6 of them, and in every draw some expert is named by exactly 6 in some block.
All inputs are finite; a program needn't handle non-finite values.
Results may differ from the reference program's by a relative error of at most 0.015.
Values may be sent and summed in bfloat16 or wider, within the bound.
No kernel may reach another device: no remote copies, remote signals or barrier semaphores. Data moves between devices by JAX's collectives and lax.ppermute only.
A program may use at most 128 MiB of HBM per device.

```python
import math
import jax
import jax.numpy as jnp
import numpy as np
from jax import lax

D = 4096
HEADS = 32
KV_HEADS = 2
HEAD_DIM = 128
FF = 768
TOPK = 4
SEQS = 1
TOK_DEV = 128
EXPERTS = 128
TOKENS = 16384
CAP = 6
N_CTX = 16
N_TP = 8


def draw_keys(key, part):
    key = jax.random.fold_in(key, 3)
    full_shape = (TOKENS, KV_HEADS * HEAD_DIM)
    drawn = jnp.clip(jax.random.normal(key, full_shape, jnp.float32), -6.0, 6.0)
    return drawn.astype(jnp.bfloat16)


def draw_queries(key, part):
    key = jax.random.fold_in(key, 5)
    full_shape = (TOKENS, HEADS * HEAD_DIM)
    drawn = jnp.clip(2.5 * jax.random.normal(key, full_shape, jnp.float32), -15.0, 15.0)
    return drawn.astype(jnp.bfloat16)


def steps_of(stream_key, shape, cuts, least, top_value):
    def one(dim, blocks):
        draws = jax.random.uniform(jax.random.fold_in(jax.random.fold_in(stream_key, 6), dim), (blocks,), jnp.float32, least / len(cuts), top_value / len(cuts))
        return jnp.repeat(jnp.exp(draws), shape[dim] // blocks).reshape((-1,) + (1,) * (len(shape) - dim - 1))

    gain = one(*cuts[0])
    for cut in cuts[1:]:
        gain = gain * one(*cut)
    return gain


def routed_block(key, own, number, rows, number_of, top, limit, lean):
    order = jax.random.permutation(key, number_of)
    crowded, usual = portions_of(number_of, rows * top, limit, lean, True), portions_of(number_of, rows * top, limit, lean, False)
    places = jnp.arange(number_of)

    def named(tallies, offset_by):
        used = int((tallies > 0).sum())
        fixed = max(1, used // 4)
        passed = fixed + (places - fixed + offset_by * (used - fixed)) % max(1, number_of - fixed)
        return jnp.zeros((number_of,), jnp.int32).at[order[jnp.where(places < fixed, places, passed)]].set(jnp.asarray(tallies, jnp.int32))

    tallies = jnp.where(number % 4 == 0, named(crowded, number // 4), named(usual, number - number // 4 - 1))
    mixed = jax.random.permutation(jax.random.fold_in(own, 3), number_of)
    donor, receiver = mixed[0:number_of // 2 * 2:2], mixed[1:number_of // 2 * 2:2]
    margin = jnp.minimum(tallies[donor] - 1, limit - tallies[receiver]) // 2
    margin = jnp.where((donor == order[0]) | (receiver == order[0]) | (tallies[receiver] == 0), 0, jnp.maximum(margin, 0))
    passed = jax.random.randint(jax.random.fold_in(own, 4), (number_of // 2,), 0, 1 << 20) % (margin + 1)
    tallies = tallies.at[donor].add(-passed).at[receiver].add(passed)
    members = jnp.searchsorted(jnp.cumsum(tallies), jnp.arange(rows * top), side="right").astype(jnp.int32)
    listing = members.reshape(top, rows).T
    listing = listing[jax.random.permutation(jax.random.fold_in(own, 1), rows)]
    offset_by = jax.random.randint(jax.random.fold_in(own, 2), (rows, 1), 0, top)
    return jnp.take_along_axis(listing, (jnp.arange(top)[None, :] + offset_by) % top, axis=1)


def portions_of(count, total, most, slope, full):
    loads = [(1 << 20) // math.isqrt(standing ** slope) + 1 for standing in range(1, count + 1)]
    largest = most if full else min(most, max(-(-total // count), total * loads[0] // sum(loads)))
    least = 1 if total - largest >= count - 1 else 0
    given, rest = [largest] + [least] * (count - 1), total - largest - least * (count - 1)
    while rest > 0:
        movable = [i for i in range(1, count) if given[i] < largest] or [i for i in range(1, count) if given[i] < most]
        pool, left = sum([loads[i] for i in movable]), rest
        for i in movable:
            extra = min(most - given[i], max(1, left * loads[i] // pool), rest)
            given[i] = given[i] + extra
            rest = rest - extra
    return np.array(given)


def normal_values(key, extent, spread, reach, cuts=(), held_as=jnp.bfloat16):
    entries = jax.random.normal(key, extent, jnp.float32) * spread
    if len(cuts) > 0:
        entries = steps_of(key, extent, cuts, -0.22, 0.18) * entries
    return jnp.clip(entries, min=-reach, max=reach).astype(held_as)


def setup_inputs(seed: int = 0) -> dict:
    streams_of = jax.random.split(jax.random.key(seed), 11)
    queries = draw_queries(jax.random.fold_in(streams_of[10], 71), 0)
    keys = draw_keys(jax.random.fold_in(streams_of[10], 71), 0)
    values = normal_values(streams_of[2], (TOKENS, KV_HEADS * HEAD_DIM), 1.0, 6.0, ((0, 16),))
    out_proj = normal_values(streams_of[3], (HEADS * HEAD_DIM, D), (HEADS * HEAD_DIM) ** -0.5, 0.09375, ((0, 8), (1, 16)))
    residual = normal_values(streams_of[4], (TOKENS, D), 1.0, 6.0, ((0, 128),))
    norm_gain = jnp.clip(1.0 + 0.18 * jax.random.normal(streams_of[5], (D,), jnp.float32), 0.1, 1.9)
    expert_ids_keys = jax.random.split(jax.random.fold_in(streams_of[6], 1), TOKENS // TOK_DEV)
    expert_ids_turns = jax.random.permutation(jax.random.fold_in(streams_of[6], 3), TOKENS // TOK_DEV)
    expert_ids = jax.vmap(lambda own, number: routed_block(jax.random.fold_in(streams_of[6], 2), own, number, TOK_DEV, EXPERTS, TOPK, CAP, 2))(expert_ids_keys, expert_ids_turns).reshape((TOKENS, TOPK))
    route_weights = jnp.clip(jnp.exp(math.log(1.0) - 2.9957323 * jax.random.uniform(streams_of[7], (TOKENS, TOPK), jnp.float32) ** steps_of(streams_of[7], (TOKENS, TOPK), ((0, 128),), -0.2, 0.2)), 0.05, 1.0)
    w_in = normal_values(streams_of[8], (EXPERTS, D, 2 * FF), D ** -0.5, 0.09375, ((0, 128),))
    w_out = normal_values(streams_of[9], (EXPERTS, FF, D), FF ** -0.5, 0.21875, ((0, 128),))
    return {"queries": queries, "keys": keys, "values": values, "out_proj": out_proj, "residual": residual, "norm_gain": norm_gain, "expert_ids": expert_ids, "route_weights": route_weights, "w_in": w_in, "w_out": w_out}


def attend_block(query_block, key_block, value_block, query_pos, key_pos):
    head_group = HEADS // KV_HEADS

    def one_head(pair):
        query_head, head_number = pair
        key_head = lax.dynamic_index_in_dim(key_block, head_number // head_group, 0, keepdims=False)
        value_head = lax.dynamic_index_in_dim(value_block, head_number // head_group, 0, keepdims=False)
        scores = jnp.dot(query_head, key_head.T, precision=lax.Precision.HIGHEST) * HEAD_DIM ** (-0.5)
        allowed = key_pos[None, :] <= query_pos[:, None]
        scores = jnp.where(allowed, scores, -1e+30)
        row_max = lax.optimization_barrier(jnp.max(scores, axis=1, keepdims=True))
        weights = jnp.where(allowed, jnp.exp(scores - row_max), 0.0)
        total = lax.optimization_barrier(jnp.sum(weights, axis=1, keepdims=True))
        rounded = lax.optimization_barrier(weights.astype(jnp.bfloat16)).astype(jnp.float32)
        return jnp.dot(rounded, value_head, precision=lax.Precision.HIGHEST) / total
    return lax.map(one_head, (query_block, jnp.arange(HEADS, dtype=jnp.int32)))

def reference(queries, keys, values, out_proj, residual, norm_gain, expert_ids, route_weights, w_in, w_out):
    seq_len = TOKENS // SEQS
    block_len = seq_len // 4
    pieces = []
    for seq_number in range(SEQS):
        key_first = seq_number * seq_len
        for block_number in range(4):
            first_row = key_first + block_number * block_len
            key_end = first_row + block_len
            query_block = queries[first_row:key_end].astype(jnp.float32).reshape(block_len, HEADS, HEAD_DIM).transpose(1, 0, 2)
            key_block = keys[key_first:key_end].astype(jnp.float32).reshape(-1, KV_HEADS, HEAD_DIM).transpose(1, 0, 2)
            value_block = values[key_first:key_end].astype(jnp.float32).reshape(-1, KV_HEADS, HEAD_DIM).transpose(1, 0, 2)
            query_pos = jnp.arange(first_row, key_end, dtype=jnp.int32)
            key_pos = jnp.arange(key_first, key_end, dtype=jnp.int32)
            result = attend_block(query_block, key_block, value_block, query_pos, key_pos)
            pieces.append(result.transpose(1, 0, 2).reshape(block_len, HEADS * HEAD_DIM).astype(jnp.bfloat16))
    attended = jnp.concatenate(pieces, axis=0)
    head_width = HEADS * HEAD_DIM // N_TP

    def add_group(total, group_number):
        first_col = (group_number * head_width).astype(jnp.int32)
        columns = lax.dynamic_slice_in_dim(attended, first_col, head_width, 1)
        proj_rows = lax.dynamic_slice_in_dim(out_proj, first_col, head_width, 0)
        partial_value = jnp.dot(columns, proj_rows, preferred_element_type=jnp.float32)
        rounded = lax.optimization_barrier(partial_value.astype(jnp.bfloat16)).astype(jnp.float32)
        return (total + rounded, None)
    attn_out, _ = lax.scan(add_group, jnp.zeros((TOKENS, D), jnp.float32), jnp.arange(N_TP, dtype=jnp.int32))
    hidden = (residual.astype(jnp.float32) + attn_out).astype(jnp.bfloat16)
    hidden_wide = hidden.astype(jnp.float32)
    variance = lax.optimization_barrier(jnp.mean(hidden_wide * hidden_wide, axis=-1, keepdims=True))
    normed = (hidden_wide * lax.rsqrt(variance + 1e-06) * norm_gain).astype(jnp.bfloat16)
    mixing = route_weights / lax.optimization_barrier(jnp.sum(route_weights, axis=-1, keepdims=True))
    route_count = TOKENS * TOPK
    per_expert = N_CTX * N_TP * CAP
    flat_ids = expert_ids.reshape(-1)
    one_hot = (flat_ids[:, None] == jnp.arange(EXPERTS, dtype=jnp.int32)[None, :]).astype(jnp.int32)
    earlier = jnp.cumsum(one_hot, axis=0) - one_hot
    slot_number = lax.optimization_barrier(jnp.sum(earlier * one_hot, axis=1))
    target = flat_ids * per_expert + slot_number
    token_of_route = jnp.arange(route_count, dtype=jnp.int32) // TOPK
    table = jnp.zeros((EXPERTS * per_expert,), jnp.int32).at[target].set(token_of_route)

    def run_expert(triple):
        rows_table, gate_up, down_weight = triple
        inputs = normed[rows_table]
        gate_up_out = jnp.dot(inputs, gate_up, preferred_element_type=jnp.float32)
        active = (jax.nn.silu(gate_up_out[:, :FF]) * gate_up_out[:, FF:]).astype(jnp.bfloat16)
        return jnp.dot(active, down_weight, preferred_element_type=jnp.float32).astype(jnp.bfloat16)
    outputs = lax.map(run_expert, (table.reshape(EXPERTS, per_expert), w_in, w_out))
    back_rows = outputs.reshape(-1, D)[target].astype(jnp.float32).reshape(TOKENS, TOPK, D)
    combined = lax.optimization_barrier(jnp.sum(mixing[:, :, None] * back_rows, axis=1))
    return (hidden_wide + combined).astype(jnp.bfloat16)
```

```python
import functools
import math

import jax
import jax.numpy as jnp
import numpy as np
from jax import lax
from jax.experimental import pallas as pl
from jax.experimental.pallas import tpu as pltpu
from jax.sharding import PartitionSpec as P

HEADS = 32
KV_HEADS = 2
HEAD_DIM = 128
FF = 768
TOPK = 4
CAP = 6
BASE2_SCALE = math.log2(math.e) / math.sqrt(HEAD_DIM)
EXPONENT_LIMIT = 100.0
KEY_WIDTH = 1024
SUB_ROWS = 256
PIECE = 512
PIECES = 8
GROUP = 8
GROUP_ROWS = GROUP * CAP
VMEM_BYTES = 56 * 2**20

VMEM_SPEC = pl.BlockSpec(memory_space=pltpu.VMEM)
SMEM_SPEC = pl.BlockSpec(memory_space=pltpu.SMEM)


def piece_swap():
    swap = np.zeros((GROUP, PIECES, CAP, PIECES, GROUP, CAP), np.float32)
    for device in range(GROUP):
        for piece in range(PIECES):
            for slot in range(CAP):
                swap[device, piece, slot, piece, device, slot] = 1
    size = GROUP * PIECES * CAP
    return jnp.asarray(swap.reshape(size, size), jnp.bfloat16)


def dot_f32(left, right):
    return jnp.dot(left, right, preferred_element_type=jnp.float32)


def dot_keys(left, keys):
    return lax.dot_general(
        left, keys, (((1,), (1,)), ((), ())), preferred_element_type=jnp.float32
    )


def attend_kernel(block_ref, q_ref, kv_ref, out_ref, q_wide, top, acc):
    rows, width, sub = q_ref.shape[0], KEY_WIDTH, SUB_ROWS
    heads = q_ref.shape[1] // HEAD_DIM
    tiles = heads * rows // sub
    block = block_ref[0]
    last = (block * rows) // width
    shift = block * rows - last * width
    bound = jnp.full((1, 1), jnp.inf, jnp.float32)
    ones = jnp.ones((width, HEAD_DIM), jnp.bfloat16)

    def load(index):
        at = pl.ds(pl.multiple_of(index * width, width), width)
        keys, values = kv_ref[at, :HEAD_DIM], kv_ref[at, HEAD_DIM:]
        return jnp.concatenate([keys, keys], 1), jnp.concatenate([values, ones], 1)

    norms = []
    for head in range(heads):
        scaled = q_ref[:, head * HEAD_DIM : (head + 1) * HEAD_DIM].astype(jnp.float32) * BASE2_SCALE
        high = scaled.astype(jnp.bfloat16)
        q_wide[head * rows : (head + 1) * rows, :HEAD_DIM] = high
        q_wide[head * rows : (head + 1) * rows, HEAD_DIM:] = (
            scaled - high.astype(jnp.float32)
        ).astype(jnp.bfloat16)
        norms.append(jnp.sqrt(jnp.sum(scaled * scaled, axis=1, keepdims=True)))

    keys, values = load(last)
    for tile in range(tiles):
        at = slice(tile * sub, (tile + 1) * sub)
        first = (tile * sub) % rows
        scores = dot_keys(q_wide[at, :], keys)
        row = lax.broadcasted_iota(jnp.int32, (sub, width), 0) + (first + shift)
        col = lax.broadcasted_iota(jnp.int32, (sub, width), 1)
        scores = jnp.where(col <= row, scores, -1e30)
        best = jnp.max(scores, axis=1, keepdims=True)
        weights = jnp.exp2(scores - best).astype(jnp.bfloat16)
        acc[at, :] = dot_f32(weights, values)
        top[at, :] = jnp.broadcast_to(best, (sub, HEAD_DIM))
        norm = norms[(tile * sub) // rows][first : first + sub]
        bound = jnp.minimum(
            bound, jnp.min((EXPONENT_LIMIT + best) / norm, axis=0, keepdims=True)
        )

    def longest(index, so_far):
        keys = kv_ref[pl.ds(pl.multiple_of(index * width, width), width), :HEAD_DIM]
        keys = keys.astype(jnp.float32)
        length = jnp.sum(keys * keys, axis=1, keepdims=True)
        return jnp.maximum(so_far, jnp.max(length, axis=0, keepdims=True))

    key_norm = jnp.sqrt(lax.fori_loop(0, last, longest, jnp.zeros((1, 1), jnp.float32)))
    safe = jnp.max(key_norm - bound) <= 0.0

    @pl.when(safe)
    def _():
        def step(index, carry):
            keys, values = load(index)
            for tile in range(tiles):
                at = slice(tile * sub, (tile + 1) * sub)
                scores = dot_keys(q_wide[at, :], keys)
                best = top[at, :]
                weights = jnp.concatenate(
                    [
                        jnp.exp2(scores[:, c : c + HEAD_DIM] - best).astype(jnp.bfloat16)
                        for c in range(0, width, HEAD_DIM)
                    ],
                    1,
                )
                acc[at, :] += dot_f32(weights, values)
            return carry

        lax.fori_loop(0, last, step, 0)

    @pl.when(jnp.logical_not(safe))
    def _():
        def step(index, carry):
            keys, values = load(index)

            def one_tile(tile, kept):
                at = pl.ds(pl.multiple_of(tile * sub, sub), sub)
                scores = dot_keys(q_wide[at, :], keys)
                old = top[at, :]
                best = jnp.maximum(old, jnp.max(scores, axis=1, keepdims=True))
                factor = jnp.exp2(old - best)
                weights = jnp.exp2(scores - best[:, :1]).astype(jnp.bfloat16)
                acc[at, :] = acc[at, :] * factor[:, :1] + dot_f32(weights, values)
                top[at, :] = best
                return kept

            return lax.fori_loop(0, tiles, one_tile, carry)

        lax.fori_loop(0, last, step, 0)

    for head in range(heads):
        at = slice(head * rows, (head + 1) * rows)
        out_ref[:, head * HEAD_DIM : (head + 1) * HEAD_DIM] = (
            acc[at, :HEAD_DIM] / acc[at, HEAD_DIM:]
        ).astype(jnp.bfloat16)


def attend(block, queries, keys_values):
    rows, columns = queries.shape
    all_rows = rows * columns // HEAD_DIM
    return pl.pallas_call(
        attend_kernel,
        out_shape=jax.ShapeDtypeStruct(queries.shape, jnp.bfloat16),
        in_specs=[SMEM_SPEC, VMEM_SPEC, VMEM_SPEC],
        out_specs=VMEM_SPEC,
        scratch_shapes=[
            pltpu.VMEM((all_rows, 2 * HEAD_DIM), jnp.bfloat16),
            pltpu.VMEM((all_rows, HEAD_DIM), jnp.float32),
            pltpu.VMEM((all_rows, 2 * HEAD_DIM), jnp.float32),
        ],
        compiler_params=pltpu.CompilerParams(vmem_limit_bytes=VMEM_BYTES),
        name="attend",
    )(block, queries, keys_values)


def dispatch_kernel(target_ref, attn_ref, residual_ref, gain_ref, swap_ref, hidden_ref, out_ref, rows_of):
    step = pl.program_id(0)

    @pl.when(step == 0)
    def _():
        hidden = (
            residual_ref[...].astype(jnp.float32) + attn_ref[...].astype(jnp.float32)
        ).astype(jnp.bfloat16)
        hidden_ref[...] = hidden
        wide = hidden.astype(jnp.float32)
        variance = jnp.mean(wide * wide, axis=-1, keepdims=True)
        normed = (wide * lax.rsqrt(variance + 1e-06) * gain_ref[...]).astype(jnp.bfloat16)
        slots, tokens = rows_of.shape[1], normed.shape[0]
        slot = lax.broadcasted_iota(jnp.int32, (slots, tokens), 0)
        chosen = jnp.zeros((slots, tokens), jnp.float32)
        for route in range(TOPK):
            chosen += jnp.where(slot == target_ref[route : route + 1, :], 1.0, 0.0)
        chosen = chosen.astype(jnp.bfloat16)
        for piece in range(PIECES):
            rows_of[piece] = dot_f32(
                chosen, normed[:, piece * PIECE : (piece + 1) * PIECE]
            ).astype(jnp.bfloat16)

    at = pl.ds(pl.multiple_of(step * GROUP_ROWS, GROUP_ROWS), GROUP_ROWS)
    stacked = jnp.concatenate([rows_of[piece, at, :] for piece in range(PIECES)], 0)
    out_ref[...] = dot_f32(swap_ref[...], stacked).astype(jnp.bfloat16)


def dispatch(target, attn_out, residual, gain, swap, dev_count):
    tokens, model = residual.shape
    slots = dev_count * CAP
    group_block = GROUP_ROWS * PIECES

    def whole(shape):
        return pl.BlockSpec(shape, lambda step: (0, 0))

    return pl.pallas_call(
        dispatch_kernel,
        grid=(dev_count // GROUP,),
        out_shape=(
            jax.ShapeDtypeStruct((tokens, model), jnp.bfloat16),
            jax.ShapeDtypeStruct((slots * PIECES, PIECE), jnp.bfloat16),
        ),
        in_specs=[
            whole((TOPK, tokens)),
            whole((tokens, model)),
            whole((tokens, model)),
            whole((1, model)),
            whole((group_block, group_block)),
        ],
        out_specs=(
            whole((tokens, model)),
            pl.BlockSpec((group_block, PIECE), lambda step: (step, 0)),
        ),
        scratch_shapes=[pltpu.VMEM((PIECES, slots, PIECE), jnp.bfloat16)],
        compiler_params=pltpu.CompilerParams(vmem_limit_bytes=VMEM_BYTES),
        name="norm_and_dispatch",
    )(target, attn_out, residual, gain, swap)


def expert_kernel(arrived_ref, swap_ref, in_ref, down_ref, out_ref, rows_of, gate_up, active):
    step = pl.program_id(0)
    groups = rows_of.shape[1] // GROUP_ROWS
    group_block = GROUP_ROWS * PIECES

    @pl.when(step == 0)
    def _():
        def unpack(group, carry):
            at = pl.ds(pl.multiple_of(group * group_block, group_block), group_block)
            stacked = dot_f32(swap_ref[...], arrived_ref[at, :]).astype(jnp.bfloat16)
            to = pl.ds(pl.multiple_of(group * GROUP_ROWS, GROUP_ROWS), GROUP_ROWS)
            for piece in range(PIECES):
                rows_of[piece, to, :] = stacked[piece * GROUP_ROWS : (piece + 1) * GROUP_ROWS]
            return carry

        lax.fori_loop(0, groups, unpack, 0, unroll=2)
        gate_up[...] = jnp.zeros_like(gate_up)

    @pl.when(step < PIECES)
    def _():
        gate_up[...] += dot_f32(rows_of[step], in_ref[...])

    @pl.when(step == PIECES - 1)
    def _():
        active[...] = (jax.nn.silu(gate_up[:, :FF]) * gate_up[:, FF:]).astype(jnp.bfloat16)

    @pl.when(step >= PIECES)
    def _():
        rows_of[step - PIECES] = dot_f32(active[...], down_ref[...]).astype(jnp.bfloat16)

    @pl.when(step == 2 * PIECES - 1)
    def _():
        def pack(group, carry):
            at = pl.ds(pl.multiple_of(group * GROUP_ROWS, GROUP_ROWS), GROUP_ROWS)
            stacked = jnp.concatenate([rows_of[piece, at, :] for piece in range(PIECES)], 0)
            to = pl.ds(pl.multiple_of(group * group_block, group_block), group_block)
            out_ref[to, :] = dot_f32(swap_ref[...], stacked).astype(jnp.bfloat16)
            return carry

        lax.fori_loop(0, groups, pack, 0, unroll=2)


def run_expert(arrived, swap, w_in, w_out):
    slots = arrived.shape[0] // PIECES
    group_block = GROUP_ROWS * PIECES
    return pl.pallas_call(
        expert_kernel,
        grid=(2 * PIECES,),
        out_shape=jax.ShapeDtypeStruct(arrived.shape, jnp.bfloat16),
        in_specs=[
            pl.BlockSpec(arrived.shape, lambda step: (0, 0)),
            pl.BlockSpec((group_block, group_block), lambda step: (0, 0)),
            pl.BlockSpec((PIECE, 2 * FF), lambda step: (jnp.minimum(step, PIECES - 1), 0)),
            pl.BlockSpec((FF, PIECE), lambda step: (0, jnp.maximum(step - PIECES, 0))),
        ],
        out_specs=pl.BlockSpec(arrived.shape, lambda step: (0, 0)),
        scratch_shapes=[
            pltpu.VMEM((PIECES, slots, PIECE), jnp.bfloat16),
            pltpu.VMEM((slots, 2 * FF), jnp.float32),
            pltpu.VMEM((slots, FF), jnp.bfloat16),
        ],
        compiler_params=pltpu.CompilerParams(vmem_limit_bytes=VMEM_BYTES),
        name="expert",
    )(arrived, swap, w_in, w_out)


def combine_kernel(target_ref, route_ref, hidden_ref, swap_ref, back_ref, out_ref, rows_of):
    step = pl.program_id(0)
    stacked = dot_f32(swap_ref[...], back_ref[...]).astype(jnp.bfloat16)
    to = pl.ds(pl.multiple_of(step * GROUP_ROWS, GROUP_ROWS), GROUP_ROWS)
    for piece in range(PIECES):
        rows_of[piece, to, :] = stacked[piece * GROUP_ROWS : (piece + 1) * GROUP_ROWS]

    @pl.when(step == pl.num_programs(0) - 1)
    def _():
        slots, tokens = rows_of.shape[1], hidden_ref.shape[0]
        route = route_ref[...]
        mixing = route / jnp.sum(route, axis=-1, keepdims=True)
        slot = lax.broadcasted_iota(jnp.int32, (tokens, slots), 1)
        spread = jnp.zeros((tokens, slots), jnp.float32)
        for number in range(TOPK):
            spread += jnp.where(
                slot == target_ref[:, number : number + 1], mixing[:, number : number + 1], 0.0
            )
        high = spread.astype(jnp.bfloat16)
        low = (spread - high.astype(jnp.float32)).astype(jnp.bfloat16)
        both = jnp.concatenate([high, low], 0)
        for piece in range(PIECES):
            columns = slice(piece * PIECE, (piece + 1) * PIECE)
            mixed = dot_f32(both, rows_of[piece])
            out_ref[:, columns] = (
                hidden_ref[:, columns].astype(jnp.float32) + mixed[:tokens] + mixed[tokens:]
            ).astype(jnp.bfloat16)


def combine(target, route_weights, hidden, swap, back):
    tokens, model = hidden.shape
    slots = back.shape[0] // PIECES
    group_block = GROUP_ROWS * PIECES

    def whole(shape):
        return pl.BlockSpec(shape, lambda step: (0, 0))

    return pl.pallas_call(
        combine_kernel,
        grid=(slots // GROUP_ROWS,),
        out_shape=jax.ShapeDtypeStruct((tokens, model), jnp.bfloat16),
        in_specs=[
            whole((tokens, TOPK)),
            whole((tokens, TOPK)),
            whole((tokens, model)),
            whole((group_block, group_block)),
            pl.BlockSpec((group_block, PIECE), lambda step: (step, 0)),
        ],
        out_specs=whole((tokens, model)),
        scratch_shapes=[pltpu.VMEM((PIECES, slots, PIECE), jnp.bfloat16)],
        compiler_params=pltpu.CompilerParams(vmem_limit_bytes=VMEM_BYTES),
        name="combine",
    )(target, route_weights, hidden, swap, back)


def body(
    queries, keys, values, out_proj, residual, norm_gain, expert_ids, route_weights, w_in, w_out
):
    ctx_count = lax.axis_size("ctx")
    dev_count = ctx_count * lax.axis_size("tp")
    ctx_index = lax.axis_index("ctx")
    heads_here = queries.shape[1] // HEAD_DIM
    kv_index = lax.axis_index("tp") * heads_here // (HEADS // KV_HEADS)
    half = queries.shape[0] // 2

    flat_ids = expert_ids.reshape(-1)
    one_hot = (flat_ids[:, None] == jnp.arange(dev_count, dtype=jnp.int32)[None, :]).astype(
        jnp.int32
    )
    earlier = jnp.cumsum(one_hot, axis=0) - one_hot
    target = (flat_ids * CAP + jnp.sum(earlier * one_hot, axis=1)).reshape(expert_ids.shape)
    swap = piece_swap()

    opposite = [(i, ctx_count - 1 - i) for i in range(ctx_count)]
    swapped = lax.ppermute(queries[half:], "ctx", opposite)
    own_kv = jnp.concatenate(
        [
            lax.dynamic_slice_in_dim(keys, kv_index * HEAD_DIM, HEAD_DIM, 1),
            lax.dynamic_slice_in_dim(values, kv_index * HEAD_DIM, HEAD_DIM, 1),
        ],
        1,
    )
    all_kv = lax.all_gather(own_kv, "ctx", axis=0, tiled=True)
    full_proj = lax.all_gather(out_proj, "ctx", axis=1, tiled=True)
    far_block = (2 * ctx_count - 1 - 2 * ctx_index).astype(jnp.int32).reshape(1)
    near_block = (2 * ctx_index).astype(jnp.int32).reshape(1)
    far = attend(far_block, swapped, all_kv)
    returned = lax.ppermute(far, "ctx", opposite)
    near = attend(near_block, queries[:half], all_kv)
    attended = jnp.concatenate([near, returned], 0)
    attn_out = lax.psum_scatter(
        dot_f32(attended, full_proj).astype(jnp.bfloat16), "tp", scatter_dimension=0, tiled=True
    )

    hidden, packed = dispatch(
        target.T, attn_out, residual, norm_gain.reshape(1, -1), swap, dev_count
    )

    def exchange(rows):
        shaped = rows.reshape(dev_count, CAP * PIECES, PIECE)
        return lax.all_to_all(
            shaped, ("ctx", "tp"), split_axis=0, concat_axis=0, tiled=True
        ).reshape(rows.shape)

    processed = run_expert(exchange(packed), swap, w_in[0], w_out[0])
    return combine(target, route_weights, hidden, swap, exchange(processed))


def solution(mesh):
    return jax.shard_map(
        body,
        mesh=mesh,
        in_specs=(
            P("ctx", "tp"),
            P("ctx", None),
            P("ctx", None),
            P("tp", "ctx"),
            P(("ctx", "tp"), None),
            P(),
            P(("ctx", "tp"), None),
            P(("ctx", "tp"), None),
            P(("ctx", "tp"), None, None),
            P(("ctx", "tp"), None, None),
        ),
        out_specs=P(("ctx", "tp"), None),
        check_vma=False,
    )
```

```python
import functools
import math

import jax
import jax.numpy as jnp
import numpy as np
from jax import lax
from jax.experimental import pallas as pl
from jax.experimental.pallas import tpu as pltpu
from jax.sharding import PartitionSpec as P

HEADS = 32
KV_HEADS = 2
HEAD_DIM = 128
FF = 768
TOPK = 4
CAP = 6
BASE2_SCALE = math.log2(math.e) / math.sqrt(HEAD_DIM)
EXPONENT_LIMIT = 100.0
KEY_WIDTH = 1024
SUB_ROWS = 256
PIECE = 512
PIECES = 8
GROUP = 8
GROUP_ROWS = GROUP * CAP
STEP_GROUPS = 4
STEP_PIECES = 2
VMEM_BYTES = 56 * 2**20
ATTEND_VMEM = 24 * 2**20
PAIR_HEADS = 2

VMEM_SPEC = pl.BlockSpec(memory_space=pltpu.VMEM)
SMEM_SPEC = pl.BlockSpec(memory_space=pltpu.SMEM)


def piece_swap():
    devices = GROUP // 2
    swap = np.zeros((PIECES, devices, CAP, devices, PIECES, CAP), np.float32)
    for device in range(devices):
        for piece in range(PIECES):
            for slot in range(CAP):
                swap[piece, device, slot, device, piece, slot] = 1
    size = devices * PIECES * CAP
    swap = swap.reshape(size, size)
    return jnp.asarray(np.stack([swap, swap.T]), jnp.bfloat16)


def unpack_group(swap_ref, message_ref, first, rows_of, to):
    size = swap_ref.shape[1]
    part = size // PIECES
    halves = [
        dot_f32(swap_ref[0], message_ref[pl.ds(pl.multiple_of(first + half * size, size), size), :])
        for half in range(2)
    ]
    for piece in range(PIECES):
        rows_of[piece, to, :] = jnp.concatenate(
            [half[piece * part : (piece + 1) * part] for half in halves], 0
        ).astype(jnp.bfloat16)


def pack_group(swap_ref, rows_of, at, message_ref, first):
    size = swap_ref.shape[1]
    part = size // PIECES
    pieces = [rows_of[piece, at, :].astype(jnp.float32) for piece in range(PIECES)]
    for half in range(2):
        stacked = jnp.concatenate([rows[half * part : (half + 1) * part] for rows in pieces], 0)
        message_ref[pl.ds(pl.multiple_of(first + half * size, size), size), :] = dot_f32(
            swap_ref[1], stacked.astype(jnp.bfloat16)
        ).astype(jnp.bfloat16)


def dot_f32(left, right):
    return jnp.dot(left, right, preferred_element_type=jnp.float32)


def dot_keys(left, keys):
    return lax.dot_general(
        left, keys, (((1,), (1,)), ((), ())), preferred_element_type=jnp.float32
    )


def attend_part(block, shift, q_ref, kv_ref, out_ref, q_wide, top, acc):
    rows, width, sub = q_ref.shape[0], KEY_WIDTH, SUB_ROWS
    heads = q_ref.shape[1] // HEAD_DIM
    tiles = heads * rows // sub
    last = (block * rows) // width
    bound = jnp.full((1, 1), jnp.inf, jnp.float32)
    ones = jnp.ones((width, HEAD_DIM), jnp.bfloat16)

    def load(index):
        at = pl.ds(pl.multiple_of(index * width, width), width)
        keys, values = kv_ref[at, :HEAD_DIM], kv_ref[at, HEAD_DIM:]
        return jnp.concatenate([keys, keys], 1), jnp.concatenate([values, ones], 1)

    norms = []
    for head in range(heads):
        scaled = q_ref[:, head * HEAD_DIM : (head + 1) * HEAD_DIM].astype(jnp.float32) * BASE2_SCALE
        high = scaled.astype(jnp.bfloat16)
        q_wide[head * rows : (head + 1) * rows, :HEAD_DIM] = high
        q_wide[head * rows : (head + 1) * rows, HEAD_DIM:] = (
            scaled - high.astype(jnp.float32)
        ).astype(jnp.bfloat16)
        norms.append(jnp.sqrt(jnp.sum(scaled * scaled, axis=1, keepdims=True)))

    keys, values = load(last)
    for tile in range(tiles):
        at = slice(tile * sub, (tile + 1) * sub)
        first = (tile * sub) % rows
        seen = shift + first + sub
        scores = dot_keys(q_wide[at, :], keys[:seen])
        row = lax.broadcasted_iota(jnp.int32, (sub, seen), 0) + (first + shift)
        col = lax.broadcasted_iota(jnp.int32, (sub, seen), 1)
        scores = jnp.where(col <= row, scores, -1e30)
        best = jnp.max(scores, axis=1, keepdims=True)
        weights = jnp.exp2(scores - best).astype(jnp.bfloat16)
        acc[at, :] = dot_f32(weights, values[:seen])
        top[at, :] = jnp.broadcast_to(best, (sub, HEAD_DIM))
        norm = norms[(tile * sub) // rows][first : first + sub]
        bound = jnp.minimum(
            bound, jnp.min((EXPONENT_LIMIT + best) / norm, axis=0, keepdims=True)
        )

    def longest(index, so_far):
        keys = kv_ref[pl.ds(pl.multiple_of(index * width, width), width), :HEAD_DIM]
        keys = keys.astype(jnp.float32)
        length = jnp.sum(keys * keys, axis=1, keepdims=True)
        return jnp.maximum(so_far, jnp.max(length, axis=0, keepdims=True))

    key_norm = jnp.sqrt(lax.fori_loop(0, last, longest, jnp.zeros((1, 1), jnp.float32)))
    safe = jnp.max(key_norm - bound) <= 0.0

    @pl.when(safe)
    def _():
        def step(index, carry):
            keys, values = load(index)
            for tile in range(tiles):
                at = slice(tile * sub, (tile + 1) * sub)
                scores = dot_keys(q_wide[at, :], keys)
                best = top[at, :]
                weights = jnp.concatenate(
                    [
                        jnp.exp2(scores[:, c : c + HEAD_DIM] - best).astype(jnp.bfloat16)
                        for c in range(0, width, HEAD_DIM)
                    ],
                    1,
                )
                acc[at, :] += dot_f32(weights, values)
            return carry

        lax.fori_loop(0, last, step, 0)

    @pl.when(jnp.logical_not(safe))
    def _():
        def step(index, carry):
            keys, values = load(index)

            def one_tile(tile, kept):
                at = pl.ds(pl.multiple_of(tile * sub, sub), sub)
                scores = dot_keys(q_wide[at, :], keys)
                old = top[at, :]
                best = jnp.maximum(old, jnp.max(scores, axis=1, keepdims=True))
                factor = jnp.exp2(old - best)
                weights = jnp.exp2(scores - best[:, :1]).astype(jnp.bfloat16)
                acc[at, :] = acc[at, :] * factor[:, :1] + dot_f32(weights, values)
                top[at, :] = best
                return kept

            return lax.fori_loop(0, tiles, one_tile, carry)

        lax.fori_loop(0, last, step, 0)

    for head in range(heads):
        at = slice(head * rows, (head + 1) * rows)
        out_ref[:, head * HEAD_DIM : (head + 1) * HEAD_DIM] = (
            acc[at, :HEAD_DIM] / acc[at, HEAD_DIM:]
        ).astype(jnp.bfloat16)


def attend_kernel(block_ref, far_ref, near_ref, kv_ref, far_out, near_out, q_wide, top, acc):
    rows = near_ref.shape[0]
    attend_part(block_ref[0], rows, far_ref, kv_ref, far_out, q_wide, top, acc)
    attend_part(block_ref[1], 0, near_ref, kv_ref, near_out, q_wide, top, acc)


def attend(blocks, far, near, keys_values):
    rows, columns = near.shape
    all_rows = rows * columns // HEAD_DIM
    result = jax.ShapeDtypeStruct((rows, columns), jnp.bfloat16)
    return pl.pallas_call(
        attend_kernel,
        out_shape=(result, result),
        in_specs=[SMEM_SPEC, VMEM_SPEC, VMEM_SPEC, VMEM_SPEC],
        out_specs=(VMEM_SPEC, VMEM_SPEC),
        scratch_shapes=[
            pltpu.VMEM((all_rows, 2 * HEAD_DIM), jnp.bfloat16),
            pltpu.VMEM((all_rows, HEAD_DIM), jnp.float32),
            pltpu.VMEM((all_rows, 2 * HEAD_DIM), jnp.float32),
        ],
        compiler_params=pltpu.CompilerParams(vmem_limit_bytes=ATTEND_VMEM),
        name="attend",
    )(blocks, far, near, keys_values)


def dispatch_kernel(target_ref, attn_ref, residual_ref, gain_ref, swap_ref, hidden_ref, out_ref, rows_of):
    step = pl.program_id(0)

    @pl.when(step == 0)
    def _():
        hidden = (
            residual_ref[...].astype(jnp.float32) + attn_ref[...].astype(jnp.float32)
        ).astype(jnp.bfloat16)
        hidden_ref[...] = hidden
        wide = hidden.astype(jnp.float32)
        variance = jnp.mean(wide * wide, axis=-1, keepdims=True)
        normed = (wide * lax.rsqrt(variance + 1e-06) * gain_ref[...]).astype(jnp.bfloat16)
        slots, tokens = rows_of.shape[1], normed.shape[0]
        slot = lax.broadcasted_iota(jnp.int32, (slots, tokens), 0)
        chosen = jnp.zeros((slots, tokens), jnp.float32)
        for route in range(TOPK):
            chosen += jnp.where(slot == target_ref[route : route + 1, :], 1.0, 0.0)
        chosen = chosen.astype(jnp.bfloat16)
        for piece in range(PIECES):
            rows_of[piece] = dot_f32(
                chosen, normed[:, piece * PIECE : (piece + 1) * PIECE]
            ).astype(jnp.bfloat16)

    group_block = GROUP_ROWS * PIECES
    for part in range(STEP_GROUPS):
        at = (step * STEP_GROUPS + part) * GROUP_ROWS
        at = pl.ds(pl.multiple_of(at, GROUP_ROWS), GROUP_ROWS)
        pack_group(swap_ref, rows_of, at, out_ref, part * group_block)


def dispatch(target, attn_out, residual, gain, swap, dev_count):
    tokens, model = residual.shape
    slots = dev_count * CAP
    group_block = GROUP_ROWS * PIECES

    def whole(shape):
        return pl.BlockSpec(shape, lambda step: (0, 0))

    return pl.pallas_call(
        dispatch_kernel,
        grid=(dev_count // (GROUP * STEP_GROUPS),),
        out_shape=(
            jax.ShapeDtypeStruct((tokens, model), jnp.bfloat16),
            jax.ShapeDtypeStruct((slots * PIECES, PIECE), jnp.bfloat16),
        ),
        in_specs=[
            whole((TOPK, tokens)),
            whole((tokens, model)),
            whole((tokens, model)),
            whole((1, model)),
            pl.BlockSpec(swap.shape, lambda step: (0, 0, 0)),
        ],
        out_specs=(
            whole((tokens, model)),
            pl.BlockSpec((STEP_GROUPS * group_block, PIECE), lambda step: (step, 0)),
        ),
        scratch_shapes=[pltpu.VMEM((PIECES, slots, PIECE), jnp.bfloat16)],
        compiler_params=pltpu.CompilerParams(vmem_limit_bytes=VMEM_BYTES),
        name="norm_and_dispatch",
    )(target, attn_out, residual, gain, swap)


def expert_kernel(arrived_ref, swap_ref, in_ref, down_ref, out_ref, rows_of, gate_up, active):
    step = pl.program_id(0)
    half = pl.num_programs(0) // 2
    groups = rows_of.shape[1] // GROUP_ROWS
    group_block = GROUP_ROWS * PIECES

    @pl.when(step == 0)
    def _():
        def unpack(group, carry):
            to = pl.ds(pl.multiple_of(group * GROUP_ROWS, GROUP_ROWS), GROUP_ROWS)
            unpack_group(swap_ref, arrived_ref, group * group_block, rows_of, to)
            return carry

        lax.fori_loop(0, groups, unpack, 0, unroll=4)

    def product():
        first = step * STEP_PIECES
        rows = jnp.concatenate([rows_of[first + part] for part in range(STEP_PIECES)], 1)
        return dot_f32(rows, in_ref[...])

    @pl.when(step == 0)
    def _():
        gate_up[...] = product()

    @pl.when((step > 0) & (step < half))
    def _():
        gate_up[...] += product()

    @pl.when(step == half - 1)
    def _():
        active[...] = (jax.nn.silu(gate_up[:, :FF]) * gate_up[:, FF:]).astype(jnp.bfloat16)

    @pl.when(step >= half)
    def _():
        first = (step - half) * STEP_PIECES
        for part in range(STEP_PIECES):
            rows_of[first + part] = dot_f32(
                active[...], down_ref[:, part * PIECE : (part + 1) * PIECE]
            ).astype(jnp.bfloat16)

    @pl.when(step == 2 * half - 1)
    def _():
        def pack(group, carry):
            at = pl.ds(pl.multiple_of(group * GROUP_ROWS, GROUP_ROWS), GROUP_ROWS)
            pack_group(swap_ref, rows_of, at, out_ref, group * group_block)
            return carry

        lax.fori_loop(0, groups, pack, 0, unroll=4)


def run_expert(arrived, swap, w_in, w_out):
    slots = arrived.shape[0] // PIECES
    group_block = GROUP_ROWS * PIECES
    half = PIECES // STEP_PIECES
    width = STEP_PIECES * PIECE
    return pl.pallas_call(
        expert_kernel,
        grid=(2 * half,),
        out_shape=jax.ShapeDtypeStruct(arrived.shape, jnp.bfloat16),
        in_specs=[
            pl.BlockSpec(arrived.shape, lambda step: (0, 0), pipeline_mode=pl.Buffered(1)),
            pl.BlockSpec(swap.shape, lambda step: (0, 0, 0)),
            pl.BlockSpec((width, 2 * FF), lambda step: (jnp.minimum(step, half - 1), 0)),
            pl.BlockSpec((FF, width), lambda step: (0, jnp.maximum(step - half, 0))),
        ],
        out_specs=pl.BlockSpec(arrived.shape, lambda step: (0, 0), pipeline_mode=pl.Buffered(1)),
        scratch_shapes=[
            pltpu.VMEM((PIECES, slots, PIECE), jnp.bfloat16),
            pltpu.VMEM((slots, 2 * FF), jnp.float32),
            pltpu.VMEM((slots, FF), jnp.bfloat16),
        ],
        compiler_params=pltpu.CompilerParams(vmem_limit_bytes=VMEM_BYTES),
        name="expert",
    )(arrived, swap, w_in, w_out)


def combine_kernel(target_ref, route_ref, hidden_ref, swap_ref, back_ref, out_ref, rows_of):
    step = pl.program_id(0)
    group_block = GROUP_ROWS * PIECES
    for part in range(STEP_GROUPS):
        to = (step * STEP_GROUPS + part) * GROUP_ROWS
        to = pl.ds(pl.multiple_of(to, GROUP_ROWS), GROUP_ROWS)
        unpack_group(swap_ref, back_ref, part * group_block, rows_of, to)

    @pl.when(step == pl.num_programs(0) - 1)
    def _():
        slots, tokens = rows_of.shape[1], hidden_ref.shape[0]
        route = route_ref[...]
        mixing = route / jnp.sum(route, axis=-1, keepdims=True)
        slot = lax.broadcasted_iota(jnp.int32, (tokens, slots), 1)
        spread = jnp.zeros((tokens, slots), jnp.float32)
        for number in range(TOPK):
            spread += jnp.where(
                slot == target_ref[:, number : number + 1], mixing[:, number : number + 1], 0.0
            )
        high = spread.astype(jnp.bfloat16)
        low = (spread - high.astype(jnp.float32)).astype(jnp.bfloat16)
        both = jnp.concatenate([high, low], 0)
        for piece in range(PIECES):
            columns = slice(piece * PIECE, (piece + 1) * PIECE)
            mixed = dot_f32(both, rows_of[piece])
            out_ref[:, columns] = (
                hidden_ref[:, columns].astype(jnp.float32) + mixed[:tokens] + mixed[tokens:]
            ).astype(jnp.bfloat16)


def combine(target, route_weights, hidden, swap, back):
    tokens, model = hidden.shape
    slots = back.shape[0] // PIECES
    group_block = GROUP_ROWS * PIECES

    def whole(shape):
        return pl.BlockSpec(shape, lambda step: (0, 0))

    return pl.pallas_call(
        combine_kernel,
        grid=(slots // (GROUP_ROWS * STEP_GROUPS),),
        out_shape=jax.ShapeDtypeStruct((tokens, model), jnp.bfloat16),
        in_specs=[
            whole((tokens, TOPK)),
            whole((tokens, TOPK)),
            whole((tokens, model)),
            pl.BlockSpec(swap.shape, lambda step: (0, 0, 0)),
            pl.BlockSpec((STEP_GROUPS * group_block, PIECE), lambda step: (step, 0)),
        ],
        out_specs=whole((tokens, model)),
        scratch_shapes=[pltpu.VMEM((PIECES, slots, PIECE), jnp.bfloat16)],
        compiler_params=pltpu.CompilerParams(vmem_limit_bytes=VMEM_BYTES),
        name="combine",
    )(target, route_weights, hidden, swap, back)


def body(
    queries, keys, values, out_proj, residual, norm_gain, expert_ids, route_weights, w_in, w_out
):
    ctx_count = lax.axis_size("ctx")
    dev_count = ctx_count * lax.axis_size("tp")
    ctx_index = lax.axis_index("ctx")
    heads_here = queries.shape[1] // HEAD_DIM
    kv_index = lax.axis_index("tp") * heads_here // (HEADS // KV_HEADS)
    half = queries.shape[0] // 2

    flat_ids = expert_ids.reshape(-1)
    one_hot = (flat_ids[:, None] == jnp.arange(dev_count, dtype=jnp.int32)[None, :]).astype(
        jnp.int32
    )
    earlier = jnp.cumsum(one_hot, axis=0) - one_hot
    target = (flat_ids * CAP + jnp.sum(earlier * one_hot, axis=1)).reshape(expert_ids.shape)
    swap = piece_swap()

    opposite = [(i, ctx_count - 1 - i) for i in range(ctx_count)]
    swapped = lax.ppermute(queries[half:], "ctx", opposite)
    own_kv = jnp.concatenate(
        [
            lax.dynamic_slice_in_dim(keys, kv_index * HEAD_DIM, HEAD_DIM, 1),
            lax.dynamic_slice_in_dim(values, kv_index * HEAD_DIM, HEAD_DIM, 1),
        ],
        1,
    )
    all_kv = lax.all_gather(own_kv, "ctx", axis=0, tiled=True)
    full_proj = lax.all_gather(out_proj, "ctx", axis=1, tiled=True)
    blocks = jnp.stack([2 * ctx_count - 1 - 2 * ctx_index, 2 * ctx_index]).astype(jnp.int32)
    nears, returned = [], []
    for first in range(0, heads_here, PAIR_HEADS):
        pair = slice(first * HEAD_DIM, (first + PAIR_HEADS) * HEAD_DIM)
        far, near = attend(blocks, swapped[:, pair], queries[:half, pair], all_kv)
        nears.append(near)
        returned.append(lax.ppermute(far, "ctx", opposite))
    attended = jnp.concatenate(
        [jnp.concatenate(nears, 1), jnp.concatenate(returned, 1)], 0
    )
    attn_out = lax.psum_scatter(
        dot_f32(attended, full_proj).astype(jnp.bfloat16), "tp", scatter_dimension=0, tiled=True
    )

    hidden, packed = dispatch(
        target.T, attn_out, residual, norm_gain.reshape(1, -1), swap, dev_count
    )

    def exchange(rows):
        shaped = rows.reshape(dev_count, CAP * PIECES, PIECE)
        return lax.all_to_all(
            shaped, ("ctx", "tp"), split_axis=0, concat_axis=0, tiled=True
        ).reshape(rows.shape)

    processed = run_expert(exchange(packed), swap, w_in[0], w_out[0])
    return combine(target, route_weights, hidden, swap, exchange(processed))


def solution(mesh):
    return jax.shard_map(
        body,
        mesh=mesh,
        in_specs=(
            P("ctx", "tp"),
            P("ctx", None),
            P("ctx", None),
            P("tp", "ctx"),
            P(("ctx", "tp"), None),
            P(),
            P(("ctx", "tp"), None),
            P(("ctx", "tp"), None),
            P(("ctx", "tp"), None, None),
            P(("ctx", "tp"), None, None),
        ),
        out_specs=P(("ctx", "tp"), None),
        check_vma=False,
    )
```

```python
import functools
import math

import jax
import jax.numpy as jnp
import numpy as np
from jax import lax
from jax.experimental import pallas as pl
from jax.experimental.pallas import tpu as pltpu
from jax.sharding import PartitionSpec as P

HEADS = 32
KV_HEADS = 2
HEAD_DIM = 128
FF = 768
TOPK = 4
CAP = 6
BASE2_SCALE = math.log2(math.e) / math.sqrt(HEAD_DIM)
EXPONENT_LIMIT = 100.0
KEY_WIDTH = 1024
SUB_ROWS = 512
WIDE_ROWS = 2048
PIECE = 512
PIECES = 8
GROUP = 8
GROUP_ROWS = GROUP * CAP
STEP_GROUPS = 4
STEP_PIECES = 2
VMEM_BYTES = 56 * 2**20
EXPERT_VMEM = 46 * 2**20
ATTEND_VMEM = 44 * 2**20

VMEM_SPEC = pl.BlockSpec(memory_space=pltpu.VMEM)
SMEM_SPEC = pl.BlockSpec(memory_space=pltpu.SMEM)


def piece_swap():
    devices = GROUP // 2
    swap = np.zeros((PIECES, devices, CAP, devices, PIECES, CAP), np.float32)
    for device in range(devices):
        for piece in range(PIECES):
            for slot in range(CAP):
                swap[piece, device, slot, device, piece, slot] = 1
    size = devices * PIECES * CAP
    swap = swap.reshape(size, size)
    return jnp.asarray(np.stack([swap, swap.T]), jnp.bfloat16)


def unpack_group(swap_ref, message_ref, first, rows_of, to):
    size = swap_ref.shape[1]
    part = size // PIECES
    halves = [
        dot_f32(swap_ref[0], message_ref[pl.ds(pl.multiple_of(first + half * size, size), size), :])
        for half in range(2)
    ]
    for piece in range(PIECES):
        rows_of[piece, to, :] = jnp.concatenate(
            [half[piece * part : (piece + 1) * part] for half in halves], 0
        ).astype(jnp.bfloat16)


def pack_group(swap_ref, rows_of, at, message_ref, first):
    size = swap_ref.shape[1]
    part = size // PIECES
    pieces = [rows_of[piece, at, :].astype(jnp.float32) for piece in range(PIECES)]
    for half in range(2):
        stacked = jnp.concatenate([rows[half * part : (half + 1) * part] for rows in pieces], 0)
        message_ref[pl.ds(pl.multiple_of(first + half * size, size), size), :] = dot_f32(
            swap_ref[1], stacked.astype(jnp.bfloat16)
        ).astype(jnp.bfloat16)


def dot_f32(left, right):
    return jnp.dot(left, right, preferred_element_type=jnp.float32)


def dot_keys(left, keys):
    return lax.dot_general(
        left, keys, (((1,), (1,)), ((), ())), preferred_element_type=jnp.float32
    )


def attend_part(block, shift, parity, q_ref, mine_ref, other_ref, out_ref, q_wide, top, acc):
    rows, width, sub = q_ref.shape[0], KEY_WIDTH, SUB_ROWS
    heads = q_ref.shape[1] // HEAD_DIM
    tiles = heads * rows // sub
    last = (block * rows) // width
    bound = jnp.full((1, 1), jnp.inf, jnp.float32)
    ones = jnp.ones((acc.shape[0] - HEAD_DIM, width), jnp.bfloat16)

    def load(index, ordered=False):
        at = pl.ds(pl.multiple_of(index * (width // 2), width // 2), width // 2)
        first, second = mine_ref[at, :], other_ref[at, :]
        if ordered:
            swapped = parity > 0
            first, second = jnp.where(swapped, second, first), jnp.where(swapped, first, second)
        both = jnp.concatenate([first, second], 0)
        keys, values = both[:, :HEAD_DIM], both[:, HEAD_DIM:]
        return jnp.concatenate([keys, keys], 1), jnp.concatenate([values.T, ones], 0)

    norms = []
    for head in range(heads):
        scaled = q_ref[:, head * HEAD_DIM : (head + 1) * HEAD_DIM].astype(jnp.float32) * BASE2_SCALE
        high = scaled.astype(jnp.bfloat16)
        q_wide[head * rows : (head + 1) * rows, :HEAD_DIM] = high
        q_wide[head * rows : (head + 1) * rows, HEAD_DIM:] = (
            scaled - high.astype(jnp.float32)
        ).astype(jnp.bfloat16)
        norms.append(jnp.max(jnp.sum(scaled * scaled, axis=1, keepdims=True), axis=0, keepdims=True))
    longest_query = jnp.sqrt(functools.reduce(jnp.maximum, norms))

    keys, values = load(last, ordered=True)
    least = jnp.full((1, sub), jnp.inf, jnp.float32)
    for tile in range(tiles):
        at = slice(tile * sub, (tile + 1) * sub)
        first = (tile * sub) % rows
        seen = shift + first + sub
        scores = dot_keys(keys[:seen], q_wide[at, :])
        key = lax.broadcasted_iota(jnp.int32, (seen, sub), 0)
        row = lax.broadcasted_iota(jnp.int32, (seen, sub), 1) + (first + shift)
        scores = jnp.where(key <= row, scores, -1e30)
        best = jnp.max(scores, axis=0, keepdims=True)
        weights = jnp.exp2(scores - best).astype(jnp.bfloat16)
        acc[:, at] = dot_f32(values[:, :seen], weights)
        top[:, at] = jnp.broadcast_to(best, (top.shape[0], sub))
        least = jnp.minimum(least, best)
    bound = (EXPONENT_LIMIT + jnp.min(least, axis=1, keepdims=True)) / longest_query

    def longest(index, so_far):
        at = pl.ds(pl.multiple_of(index * (width // 2), width // 2), width // 2)
        for held in (mine_ref, other_ref):
            keys = held[at, :HEAD_DIM].astype(jnp.float32)
            length = jnp.sum(keys * keys, axis=1, keepdims=True)
            so_far = jnp.maximum(so_far, jnp.max(length, axis=0, keepdims=True))
        return so_far

    key_norm = jnp.sqrt(lax.fori_loop(0, last, longest, jnp.zeros((1, 1), jnp.float32)))
    safe = jnp.max(key_norm - bound) <= 0.0

    @pl.when(safe)
    def _():
        def step(index, carry):
            keys, values = load(index)
            for first in range(0, heads * rows, WIDE_ROWS):
                at = slice(first, first + WIDE_ROWS)
                scores = dot_keys(keys, q_wide[at, :])
                weights = jnp.exp2(scores - top[:1, at]).astype(jnp.bfloat16)
                acc[:, at] += dot_f32(values, weights)
            return carry

        lax.fori_loop(0, last, step, 0)

    @pl.when(jnp.logical_not(safe))
    def _():
        def step(index, carry):
            keys, values = load(index)
            for tile in range(tiles):
                at = slice(tile * sub, (tile + 1) * sub)
                scores = dot_keys(keys, q_wide[at, :])
                old = top[:1, at]
                best = jnp.maximum(old, jnp.max(scores, axis=0, keepdims=True))
                weights = jnp.exp2(scores - best).astype(jnp.bfloat16)
                acc[:, at] = acc[:, at] * jnp.exp2(old - best) + dot_f32(values, weights)
                top[:, at] = jnp.broadcast_to(best, (top.shape[0], sub))
            return carry

        lax.fori_loop(0, last, step, 0)

    for head in range(heads):
        at = slice(head * rows, (head + 1) * rows)
        mean = acc[:HEAD_DIM, at] / acc[HEAD_DIM : HEAD_DIM + 1, at]
        out_ref[:, head * HEAD_DIM : (head + 1) * HEAD_DIM] = mean.T.astype(jnp.bfloat16)


def attend_kernel(place_ref, far_ref, near_ref, mine_ref, other_ref, far_out, near_out, *scratch):
    rows = near_ref.shape[0]
    parity = place_ref[2]
    attend_part(place_ref[0], rows, parity, far_ref, mine_ref, other_ref, far_out, *scratch)
    attend_part(place_ref[1], 0, parity, near_ref, mine_ref, other_ref, near_out, *scratch)


def attend(place, far, near, mine, other):
    rows, columns = near.shape
    all_rows = rows * columns // HEAD_DIM
    result = jax.ShapeDtypeStruct((rows, columns), jnp.bfloat16)
    return pl.pallas_call(
        attend_kernel,
        out_shape=(result, result),
        in_specs=[SMEM_SPEC] + [VMEM_SPEC] * 4,
        out_specs=(VMEM_SPEC, VMEM_SPEC),
        scratch_shapes=[
            pltpu.VMEM((all_rows, 2 * HEAD_DIM), jnp.bfloat16),
            pltpu.VMEM((8, all_rows), jnp.float32),
            pltpu.VMEM((HEAD_DIM + 16, all_rows), jnp.float32),
        ],
        compiler_params=pltpu.CompilerParams(vmem_limit_bytes=ATTEND_VMEM),
        name="attend",
    )(place, far, near, mine, other)


def project_kernel(attended_ref, proj_ref, *rest):
    rest[-1][...] = dot_f32(attended_ref[...], proj_ref[...]).astype(jnp.bfloat16)


def project(attended, proj, half, so_far=None):
    rows, depth = attended.shape
    model = proj.shape[1]
    width = 2 * PIECE
    operands = (attended, proj) if so_far is None else (attended, proj, so_far)
    return pl.pallas_call(
        project_kernel,
        grid=(model // width,),
        out_shape=jax.ShapeDtypeStruct((2 * rows, model), jnp.bfloat16),
        in_specs=[
            pl.BlockSpec((rows, depth), lambda step: (0, 0)),
            pl.BlockSpec((depth, width), lambda step: (0, step)),
            pl.BlockSpec(memory_space=pl.ANY),
        ][: len(operands)],
        out_specs=pl.BlockSpec((rows, width), lambda step: (half, step)),
        input_output_aliases={} if so_far is None else {2: 0},
        cost_estimate=pl.CostEstimate(
            flops=2 * rows * depth * model,
            bytes_accessed=2 * (rows * depth + depth * model + rows * model),
            transcendentals=0,
        ),
        compiler_params=pltpu.CompilerParams(vmem_limit_bytes=VMEM_BYTES // 2),
        name="project",
    )(*operands)


def dispatch_kernel(target_ref, attn_ref, residual_ref, gain_ref, swap_ref, hidden_ref, out_ref, rows_of):
    step = pl.program_id(0)

    @pl.when(step == 0)
    def _():
        hidden = (
            residual_ref[...].astype(jnp.float32) + attn_ref[...].astype(jnp.float32)
        ).astype(jnp.bfloat16)
        hidden_ref[...] = hidden
        wide = hidden.astype(jnp.float32)
        variance = jnp.mean(wide * wide, axis=-1, keepdims=True)
        normed = (wide * lax.rsqrt(variance + 1e-06) * gain_ref[...]).astype(jnp.bfloat16)
        slots, tokens = rows_of.shape[1], normed.shape[0]
        slot = lax.broadcasted_iota(jnp.int32, (slots, tokens), 0)
        chosen = jnp.zeros((slots, tokens), jnp.float32)
        for route in range(TOPK):
            chosen += jnp.where(slot == target_ref[route : route + 1, :], 1.0, 0.0)
        chosen = chosen.astype(jnp.bfloat16)
        for piece in range(PIECES):
            rows_of[piece] = dot_f32(
                chosen, normed[:, piece * PIECE : (piece + 1) * PIECE]
            ).astype(jnp.bfloat16)

    group_block = GROUP_ROWS * PIECES
    for part in range(STEP_GROUPS):
        at = (step * STEP_GROUPS + part) * GROUP_ROWS
        at = pl.ds(pl.multiple_of(at, GROUP_ROWS), GROUP_ROWS)
        pack_group(swap_ref, rows_of, at, out_ref, part * group_block)


def dispatch(target, attn_out, residual, gain, swap, dev_count):
    tokens, model = residual.shape
    slots = dev_count * CAP
    group_block = GROUP_ROWS * PIECES

    def whole(shape):
        return pl.BlockSpec(shape, lambda step: (0, 0))

    return pl.pallas_call(
        dispatch_kernel,
        grid=(dev_count // (GROUP * STEP_GROUPS),),
        out_shape=(
            jax.ShapeDtypeStruct((tokens, model), jnp.bfloat16),
            jax.ShapeDtypeStruct((slots * PIECES, PIECE), jnp.bfloat16),
        ),
        in_specs=[
            whole((TOPK, tokens)),
            whole((tokens, model)),
            whole((tokens, model)),
            whole((1, model)),
            pl.BlockSpec(swap.shape, lambda step: (0, 0, 0)),
        ],
        out_specs=(
            whole((tokens, model)),
            pl.BlockSpec((STEP_GROUPS * group_block, PIECE), lambda step: (step, 0)),
        ),
        scratch_shapes=[pltpu.VMEM((PIECES, slots, PIECE), jnp.bfloat16)],
        compiler_params=pltpu.CompilerParams(vmem_limit_bytes=VMEM_BYTES),
        name="norm_and_dispatch",
    )(target, attn_out, residual, gain, swap)


def expert_kernel(
    arrived_ref, swap_ref, in_hbm, down_hbm, out_ref, in_ref, down_ref, landed, rows_of, gate_up, active
):
    groups = rows_of.shape[1] // GROUP_ROWS
    group_block = GROUP_ROWS * PIECES
    steps = PIECES // STEP_PIECES
    width = STEP_PIECES * PIECE

    def columns(step):
        return slice(step * width, (step + 1) * width)

    weights_in = [
        pltpu.make_async_copy(in_hbm.at[columns(step), :], in_ref.at[columns(step), :], landed.at[0, step])
        for step in range(steps)
    ]
    weights_down = [
        pltpu.make_async_copy(
            down_hbm.at[:, columns(step)], down_ref.at[:, columns(step)], landed.at[1, step]
        )
        for step in range(steps)
    ]
    for copy in weights_in + weights_down:
        copy.start()

    def unpack(group, carry):
        to = pl.ds(pl.multiple_of(group * GROUP_ROWS, GROUP_ROWS), GROUP_ROWS)
        unpack_group(swap_ref, arrived_ref, group * group_block, rows_of, to)
        return carry

    lax.fori_loop(0, groups, unpack, 0, unroll=4)
    for step in range(steps):
        weights_in[step].wait()
        pieces = range(step * STEP_PIECES, (step + 1) * STEP_PIECES)
        rows = jnp.concatenate([rows_of[piece] for piece in pieces], 1)
        part = dot_f32(rows, in_ref[columns(step), :])
        if step == 0:
            gate_up[...] = part
        else:
            gate_up[...] += part
    active[...] = (jax.nn.silu(gate_up[:, :FF]) * gate_up[:, FF:]).astype(jnp.bfloat16)
    for step in range(steps):
        weights_down[step].wait()
        for piece in range(step * STEP_PIECES, (step + 1) * STEP_PIECES):
            rows_of[piece] = dot_f32(
                active[...], down_ref[:, piece * PIECE : (piece + 1) * PIECE]
            ).astype(jnp.bfloat16)

    def pack(group, carry):
        at = pl.ds(pl.multiple_of(group * GROUP_ROWS, GROUP_ROWS), GROUP_ROWS)
        pack_group(swap_ref, rows_of, at, out_ref, group * group_block)
        return carry

    lax.fori_loop(0, groups, pack, 0, unroll=4)


def run_expert(arrived, swap, w_in, w_out):
    slots = arrived.shape[0] // PIECES
    any_spec = pl.BlockSpec(memory_space=pl.ANY)
    return pl.pallas_call(
        expert_kernel,
        out_shape=jax.ShapeDtypeStruct(arrived.shape, jnp.bfloat16),
        in_specs=[VMEM_SPEC, VMEM_SPEC, any_spec, any_spec],
        out_specs=VMEM_SPEC,
        scratch_shapes=[
            pltpu.VMEM(w_in.shape, jnp.bfloat16),
            pltpu.VMEM(w_out.shape, jnp.bfloat16),
            pltpu.SemaphoreType.DMA((2, PIECES // STEP_PIECES)),
            pltpu.VMEM((PIECES, slots, PIECE), jnp.bfloat16),
            pltpu.VMEM((slots, 2 * FF), jnp.float32),
            pltpu.VMEM((slots, FF), jnp.bfloat16),
        ],
        compiler_params=pltpu.CompilerParams(vmem_limit_bytes=EXPERT_VMEM),
        name="expert",
    )(arrived, swap, w_in, w_out)


def combine_kernel(target_ref, route_ref, hidden_ref, swap_ref, back_ref, out_ref, rows_of):
    step = pl.program_id(0)
    group_block = GROUP_ROWS * PIECES
    for part in range(STEP_GROUPS):
        to = (step * STEP_GROUPS + part) * GROUP_ROWS
        to = pl.ds(pl.multiple_of(to, GROUP_ROWS), GROUP_ROWS)
        unpack_group(swap_ref, back_ref, part * group_block, rows_of, to)

    @pl.when(step == pl.num_programs(0) - 1)
    def _():
        slots, tokens = rows_of.shape[1], hidden_ref.shape[0]
        route = route_ref[...]
        mixing = route / jnp.sum(route, axis=-1, keepdims=True)
        slot = lax.broadcasted_iota(jnp.int32, (tokens, slots), 1)
        spread = jnp.zeros((tokens, slots), jnp.float32)
        for number in range(TOPK):
            spread += jnp.where(
                slot == target_ref[:, number : number + 1], mixing[:, number : number + 1], 0.0
            )
        high = spread.astype(jnp.bfloat16)
        low = (spread - high.astype(jnp.float32)).astype(jnp.bfloat16)
        both = jnp.concatenate([high, low], 0)
        for piece in range(PIECES):
            columns = slice(piece * PIECE, (piece + 1) * PIECE)
            mixed = dot_f32(both, rows_of[piece])
            out_ref[:, columns] = (
                hidden_ref[:, columns].astype(jnp.float32) + mixed[:tokens] + mixed[tokens:]
            ).astype(jnp.bfloat16)


def combine(target, route_weights, hidden, swap, back):
    tokens, model = hidden.shape
    slots = back.shape[0] // PIECES
    group_block = GROUP_ROWS * PIECES

    def whole(shape):
        return pl.BlockSpec(shape, lambda step: (0, 0))

    return pl.pallas_call(
        combine_kernel,
        grid=(slots // (GROUP_ROWS * STEP_GROUPS),),
        out_shape=jax.ShapeDtypeStruct((tokens, model), jnp.bfloat16),
        in_specs=[
            whole((tokens, TOPK)),
            whole((tokens, TOPK)),
            whole((tokens, model)),
            pl.BlockSpec(swap.shape, lambda step: (0, 0, 0)),
            pl.BlockSpec((STEP_GROUPS * group_block, PIECE), lambda step: (step, 0)),
        ],
        out_specs=whole((tokens, model)),
        scratch_shapes=[pltpu.VMEM((PIECES, slots, PIECE), jnp.bfloat16)],
        compiler_params=pltpu.CompilerParams(vmem_limit_bytes=VMEM_BYTES),
        name="combine",
    )(target, route_weights, hidden, swap, back)


def body(
    queries, keys, values, out_proj, residual, norm_gain, expert_ids, route_weights, w_in, w_out
):
    ctx_count = lax.axis_size("ctx")
    dev_count = ctx_count * lax.axis_size("tp")
    ctx_index = lax.axis_index("ctx")
    heads_here = queries.shape[1] // HEAD_DIM
    kv_index = lax.axis_index("tp") * heads_here // (HEADS // KV_HEADS)
    half = queries.shape[0] // 2

    flat_ids = expert_ids.reshape(-1)
    one_hot = (flat_ids[:, None] == jnp.arange(dev_count, dtype=jnp.int32)[None, :]).astype(
        jnp.int32
    )
    earlier = jnp.cumsum(one_hot, axis=0) - one_hot
    target = (flat_ids * CAP + jnp.sum(earlier * one_hot, axis=1)).reshape(expert_ids.shape)
    swap = piece_swap()

    opposite = [(i, ctx_count - 1 - i) for i in range(ctx_count)]
    swapped = lax.ppermute(queries[half:], "ctx", opposite)
    parity = lax.axis_index("tp") % 2
    column = kv_index * HEAD_DIM
    own_kv = jnp.concatenate(
        [
            lax.dynamic_slice(full, (parity * half, column), (half, HEAD_DIM))
            for full in (keys, values)
        ],
        1,
    )
    mine = lax.all_gather(own_kv, "ctx", axis=0, tiled=True)
    swapped, mine = lax.optimization_barrier((swapped, mine))
    other = lax.ppermute(mine, "tp", [(i, i ^ 1) for i in range(lax.axis_size("tp"))])
    full_proj = lax.all_gather(out_proj, "ctx", axis=1, tiled=True)
    place = jnp.stack(
        [2 * ctx_count - 1 - 2 * ctx_index, 2 * ctx_index, parity]
    ).astype(jnp.int32)
    far, near = attend(place, swapped, queries[:half], mine, other)
    returned = lax.ppermute(far, "ctx", opposite)
    projected = project(returned, full_proj, 1, project(near, full_proj, 0))
    attn_out = lax.psum_scatter(projected, "tp", scatter_dimension=0, tiled=True)

    hidden, packed = dispatch(
        target.T, attn_out, residual, norm_gain.reshape(1, -1), swap, dev_count
    )

    def exchange(rows):
        shaped = rows.reshape(dev_count, CAP * PIECES, PIECE)
        return lax.all_to_all(
            shaped, ("ctx", "tp"), split_axis=0, concat_axis=0, tiled=True
        ).reshape(rows.shape)

    processed = run_expert(exchange(packed), swap, w_in[0], w_out[0])
    return combine(target, route_weights, hidden, swap, exchange(processed))


def solution(mesh):
    return jax.shard_map(
        body,
        mesh=mesh,
        in_specs=(
            P("ctx", "tp"),
            P("ctx", None),
            P("ctx", None),
            P("tp", "ctx"),
            P(("ctx", "tp"), None),
            P(),
            P(("ctx", "tp"), None),
            P(("ctx", "tp"), None),
            P(("ctx", "tp"), None, None),
            P(("ctx", "tp"), None, None),
        ),
        out_specs=P(("ctx", "tp"), None),
        check_vma=False,
    )
```

```python
import functools
import math

import jax
import jax.numpy as jnp
import numpy as np
from jax import lax
from jax.experimental import pallas as pl
from jax.experimental.pallas import tpu as pltpu
from jax.sharding import PartitionSpec as P

HEADS = 32
KV_HEADS = 2
HEAD_DIM = 128
FF = 768
TOPK = 4
CAP = 6
BASE2_SCALE = math.log2(math.e) / math.sqrt(HEAD_DIM)
EXPONENT_LIMIT = 100.0
KEY_WIDTH = 1024
SUB_ROWS = 512
WIDE_ROWS = 2048
PIECE = 512
PIECES = 8
GROUP = 8
GROUP_ROWS = GROUP * CAP
STEP_GROUPS = 4
STEP_PIECES = 2
PROJECT_WIDTH = 2048
VMEM_BYTES = 56 * 2**20
EXPERT_VMEM = 46 * 2**20
ATTEND_VMEM = 36 * 2**20

VMEM_SPEC = pl.BlockSpec(memory_space=pltpu.VMEM)
SMEM_SPEC = pl.BlockSpec(memory_space=pltpu.SMEM)


def piece_swap():
    devices = GROUP // 2
    swap = np.zeros((PIECES, devices, CAP, devices, PIECES, CAP), np.float32)
    for device in range(devices):
        for piece in range(PIECES):
            for slot in range(CAP):
                swap[piece, device, slot, device, piece, slot] = 1
    size = devices * PIECES * CAP
    swap = swap.reshape(size, size)
    return jnp.asarray(np.stack([swap, swap.T]), jnp.bfloat16)


def unpack_group(swap_ref, message_ref, first, rows_of, to):
    size = swap_ref.shape[1]
    part = size // PIECES
    halves = [
        dot_f32(swap_ref[0], message_ref[pl.ds(pl.multiple_of(first + half * size, size), size), :])
        for half in range(2)
    ]
    for piece in range(PIECES):
        rows_of[piece, to, :] = jnp.concatenate(
            [half[piece * part : (piece + 1) * part] for half in halves], 0
        ).astype(jnp.bfloat16)


def pack_group(swap_ref, rows_of, at, message_ref, first):
    size = swap_ref.shape[1]
    part = size // PIECES
    pieces = [rows_of[piece, at, :].astype(jnp.float32) for piece in range(PIECES)]
    for half in range(2):
        stacked = jnp.concatenate([rows[half * part : (half + 1) * part] for rows in pieces], 0)
        message_ref[pl.ds(pl.multiple_of(first + half * size, size), size), :] = dot_f32(
            swap_ref[1], stacked.astype(jnp.bfloat16)
        ).astype(jnp.bfloat16)


def dot_f32(left, right):
    return jnp.dot(left, right, preferred_element_type=jnp.float32)


def dot_keys(left, keys):
    return lax.dot_general(
        left, keys, (((1,), (1,)), ((), ())), preferred_element_type=jnp.float32
    )


def own_half_kernel(place_ref, keys_ref, values_ref, out_ref):
    out_ref[:, :HEAD_DIM] = keys_ref[...]
    out_ref[:, HEAD_DIM:] = values_ref[...]


def own_half(place, keys, values, half):
    taken = pl.BlockSpec((half, HEAD_DIM), lambda step, place_ref: (place_ref[2], place_ref[3]))
    return pl.pallas_call(
        own_half_kernel,
        grid_spec=pltpu.PrefetchScalarGridSpec(
            num_scalar_prefetch=1,
            grid=(1,),
            in_specs=[taken, taken],
            out_specs=pl.BlockSpec((half, 2 * HEAD_DIM), lambda step, place_ref: (0, 0)),
        ),
        out_shape=jax.ShapeDtypeStruct((half, 2 * HEAD_DIM), jnp.bfloat16),
        name="own_half",
    )(place, keys, values)


def attend_part(block, shift, parity, q_ref, mine_ref, other_ref, out_ref, q_wide, top, acc):
    rows, width, sub = q_ref.shape[0], KEY_WIDTH, SUB_ROWS
    heads = q_ref.shape[1] // HEAD_DIM
    tiles = heads * rows // sub
    last = (block * rows) // width
    bound = jnp.full((1, 1), jnp.inf, jnp.float32)
    ones = jnp.ones((acc.shape[0] - HEAD_DIM, width), jnp.bfloat16)

    def load(index, ordered=False):
        at = pl.ds(pl.multiple_of(index * (width // 2), width // 2), width // 2)
        first, second = mine_ref[at, :], other_ref[at, :]
        if ordered:
            swapped = parity > 0
            first, second = jnp.where(swapped, second, first), jnp.where(swapped, first, second)
        both = jnp.concatenate([first, second], 0)
        keys, values = both[:, :HEAD_DIM], both[:, HEAD_DIM:]
        return jnp.concatenate([keys, keys], 1), jnp.concatenate([values.T, ones], 0)

    norms = []
    for head in range(heads):
        scaled = q_ref[:, head * HEAD_DIM : (head + 1) * HEAD_DIM].astype(jnp.float32) * BASE2_SCALE
        high = scaled.astype(jnp.bfloat16)
        q_wide[head * rows : (head + 1) * rows, :HEAD_DIM] = high
        q_wide[head * rows : (head + 1) * rows, HEAD_DIM:] = (
            scaled - high.astype(jnp.float32)
        ).astype(jnp.bfloat16)
        norms.append(jnp.max(jnp.sum(scaled * scaled, axis=1, keepdims=True), axis=0, keepdims=True))
    longest_query = jnp.sqrt(functools.reduce(jnp.maximum, norms))

    keys, values = load(last, ordered=True)
    least = jnp.full((1, sub), jnp.inf, jnp.float32)
    for tile in range(tiles):
        at = slice(tile * sub, (tile + 1) * sub)
        first = (tile * sub) % rows
        seen = shift + first + sub
        scores = dot_keys(keys[:seen], q_wide[at, :])
        key = lax.broadcasted_iota(jnp.int32, (seen, sub), 0)
        row = lax.broadcasted_iota(jnp.int32, (seen, sub), 1) + (first + shift)
        scores = jnp.where(key <= row, scores, -1e30)
        best = jnp.max(scores, axis=0, keepdims=True)
        weights = jnp.exp2(scores - best).astype(jnp.bfloat16)
        acc[:, at] = dot_f32(values[:, :seen], weights)
        top[:, at] = jnp.broadcast_to(best, (top.shape[0], sub))
        least = jnp.minimum(least, best)
    bound = (EXPONENT_LIMIT + jnp.min(least, axis=1, keepdims=True)) / longest_query

    def longest(index, so_far):
        at = pl.ds(pl.multiple_of(index * (width // 2), width // 2), width // 2)
        for held in (mine_ref, other_ref):
            keys = held[at, :HEAD_DIM].astype(jnp.float32)
            length = jnp.sum(keys * keys, axis=1, keepdims=True)
            so_far = jnp.maximum(so_far, jnp.max(length, axis=0, keepdims=True))
        return so_far

    key_norm = jnp.sqrt(lax.fori_loop(0, last, longest, jnp.zeros((1, 1), jnp.float32)))
    safe = jnp.max(key_norm - bound) <= 0.0

    @pl.when(safe)
    def _():
        def step(index, carry):
            keys, values = load(index)
            for first in range(0, heads * rows, WIDE_ROWS):
                at = slice(first, first + WIDE_ROWS)
                scores = dot_keys(keys, q_wide[at, :])
                weights = jnp.exp2(scores - top[:1, at]).astype(jnp.bfloat16)
                acc[:, at] += dot_f32(values, weights)
            return carry

        lax.fori_loop(0, last, step, 0)

    @pl.when(jnp.logical_not(safe))
    def _():
        def step(index, carry):
            keys, values = load(index)
            for tile in range(tiles):
                at = slice(tile * sub, (tile + 1) * sub)
                scores = dot_keys(keys, q_wide[at, :])
                old = top[:1, at]
                best = jnp.maximum(old, jnp.max(scores, axis=0, keepdims=True))
                weights = jnp.exp2(scores - best).astype(jnp.bfloat16)
                acc[:, at] = acc[:, at] * jnp.exp2(old - best) + dot_f32(values, weights)
                top[:, at] = jnp.broadcast_to(best, (top.shape[0], sub))
            return carry

        lax.fori_loop(0, last, step, 0)

    for head in range(heads):
        at = slice(head * rows, (head + 1) * rows)
        mean = acc[:HEAD_DIM, at] / acc[HEAD_DIM : HEAD_DIM + 1, at]
        out_ref[:, head * HEAD_DIM : (head + 1) * HEAD_DIM] = mean.T.astype(jnp.bfloat16)


def attend_kernel(place_ref, far_ref, near_ref, mine_ref, other_ref, far_out, near_out, *scratch):
    rows = near_ref.shape[0]
    parity = place_ref[2]
    attend_part(place_ref[0], rows, parity, far_ref, mine_ref, other_ref, far_out, *scratch)
    attend_part(place_ref[1], 0, parity, near_ref, mine_ref, other_ref, near_out, *scratch)


def attend(place, far, near, mine, other):
    rows, columns = near.shape
    all_rows = rows * columns // HEAD_DIM
    result = jax.ShapeDtypeStruct((rows, columns), jnp.bfloat16)
    return pl.pallas_call(
        attend_kernel,
        out_shape=(result, result),
        in_specs=[SMEM_SPEC] + [VMEM_SPEC] * 4,
        out_specs=(VMEM_SPEC, VMEM_SPEC),
        scratch_shapes=[
            pltpu.VMEM((all_rows, 2 * HEAD_DIM), jnp.bfloat16),
            pltpu.VMEM((8, all_rows), jnp.float32),
            pltpu.VMEM((HEAD_DIM + 16, all_rows), jnp.float32),
        ],
        compiler_params=pltpu.CompilerParams(vmem_limit_bytes=ATTEND_VMEM),
        name="attend",
    )(place, far, near, mine, other)


def project_kernel(attended_ref, proj_ref, *rest):
    out_ref = rest[-1]
    proj = jnp.concatenate([proj_ref[part] for part in range(proj_ref.shape[0])], 1)
    out_ref[...] = dot_f32(attended_ref[...], proj).astype(jnp.bfloat16)


def project(attended, proj, half, so_far=None):
    rows, depth = attended.shape
    parts, _, width = proj.shape
    model = parts * width
    taken = PROJECT_WIDTH // width
    operands = (attended, proj) if so_far is None else (attended, proj, so_far)
    return pl.pallas_call(
        project_kernel,
        grid=(parts // taken,),
        out_shape=jax.ShapeDtypeStruct((2 * rows, model), jnp.bfloat16),
        in_specs=[
            pl.BlockSpec((rows, depth), lambda step: (0, 0)),
            pl.BlockSpec((taken, depth, width), lambda step: (step, 0, 0)),
            pl.BlockSpec(memory_space=pl.ANY),
        ][: len(operands)],
        out_specs=pl.BlockSpec((rows, taken * width), lambda step: (half, step)),
        input_output_aliases={} if so_far is None else {2: 0},
        cost_estimate=pl.CostEstimate(
            flops=2 * rows * depth * model,
            bytes_accessed=2 * (rows * depth + depth * model + rows * model),
            transcendentals=0,
        ),
        compiler_params=pltpu.CompilerParams(vmem_limit_bytes=VMEM_BYTES),
        name="project",
    )(*operands)


def dispatch_kernel(target_ref, attn_ref, residual_ref, gain_ref, swap_ref, hidden_ref, out_ref, rows_of):
    step = pl.program_id(0)

    @pl.when(step == 0)
    def _():
        hidden = (
            residual_ref[...].astype(jnp.float32) + attn_ref[...].astype(jnp.float32)
        ).astype(jnp.bfloat16)
        hidden_ref[...] = hidden
        wide = hidden.astype(jnp.float32)
        variance = jnp.mean(wide * wide, axis=-1, keepdims=True)
        normed = (wide * lax.rsqrt(variance + 1e-06) * gain_ref[...]).astype(jnp.bfloat16)
        slots, tokens = rows_of.shape[1], normed.shape[0]
        slot = lax.broadcasted_iota(jnp.int32, (slots, tokens), 0)
        chosen = jnp.zeros((slots, tokens), jnp.float32)
        for route in range(TOPK):
            chosen += jnp.where(slot == target_ref[route : route + 1, :], 1.0, 0.0)
        chosen = chosen.astype(jnp.bfloat16)
        for piece in range(PIECES):
            rows_of[piece] = dot_f32(
                chosen, normed[:, piece * PIECE : (piece + 1) * PIECE]
            ).astype(jnp.bfloat16)

    group_block = GROUP_ROWS * PIECES
    for part in range(STEP_GROUPS):
        at = (step * STEP_GROUPS + part) * GROUP_ROWS
        at = pl.ds(pl.multiple_of(at, GROUP_ROWS), GROUP_ROWS)
        pack_group(swap_ref, rows_of, at, out_ref, part * group_block)


def dispatch(target, attn_out, residual, gain, swap, dev_count):
    tokens, model = residual.shape
    slots = dev_count * CAP
    group_block = GROUP_ROWS * PIECES

    def whole(shape):
        return pl.BlockSpec(shape, lambda step: (0, 0))

    return pl.pallas_call(
        dispatch_kernel,
        grid=(dev_count // (GROUP * STEP_GROUPS),),
        out_shape=(
            jax.ShapeDtypeStruct((tokens, model), jnp.bfloat16),
            jax.ShapeDtypeStruct((slots * PIECES, PIECE), jnp.bfloat16),
        ),
        in_specs=[
            whole((TOPK, tokens)),
            whole((tokens, model)),
            whole((tokens, model)),
            whole((1, model)),
            pl.BlockSpec(swap.shape, lambda step: (0, 0, 0)),
        ],
        out_specs=(
            whole((tokens, model)),
            pl.BlockSpec((STEP_GROUPS * group_block, PIECE), lambda step: (step, 0)),
        ),
        scratch_shapes=[pltpu.VMEM((PIECES, slots, PIECE), jnp.bfloat16)],
        compiler_params=pltpu.CompilerParams(vmem_limit_bytes=VMEM_BYTES),
        name="norm_and_dispatch",
    )(target, attn_out, residual, gain, swap)


def expert_kernel(
    arrived_ref, swap_ref, in_hbm, down_hbm, out_ref, in_ref, down_ref, landed, rows_of, gate_up, active
):
    groups = rows_of.shape[1] // GROUP_ROWS
    group_block = GROUP_ROWS * PIECES
    steps = PIECES // STEP_PIECES
    width = STEP_PIECES * PIECE

    def columns(step):
        return slice(step * width, (step + 1) * width)

    weights_in = [
        pltpu.make_async_copy(in_hbm.at[columns(step), :], in_ref.at[columns(step), :], landed.at[0, step])
        for step in range(steps)
    ]
    weights_down = [
        pltpu.make_async_copy(
            down_hbm.at[:, columns(step)], down_ref.at[:, columns(step)], landed.at[1, step]
        )
        for step in range(steps)
    ]
    for copy in weights_in + weights_down:
        copy.start()

    def unpack(group, carry):
        to = pl.ds(pl.multiple_of(group * GROUP_ROWS, GROUP_ROWS), GROUP_ROWS)
        unpack_group(swap_ref, arrived_ref, group * group_block, rows_of, to)
        return carry

    lax.fori_loop(0, groups, unpack, 0, unroll=4)
    for step in range(steps):
        weights_in[step].wait()
        pieces = range(step * STEP_PIECES, (step + 1) * STEP_PIECES)
        rows = jnp.concatenate([rows_of[piece] for piece in pieces], 1)
        part = dot_f32(rows, in_ref[columns(step), :])
        if step == 0:
            gate_up[...] = part
        else:
            gate_up[...] += part
    active[...] = (jax.nn.silu(gate_up[:, :FF]) * gate_up[:, FF:]).astype(jnp.bfloat16)
    for step in range(steps):
        weights_down[step].wait()
        for piece in range(step * STEP_PIECES, (step + 1) * STEP_PIECES):
            rows_of[piece] = dot_f32(
                active[...], down_ref[:, piece * PIECE : (piece + 1) * PIECE]
            ).astype(jnp.bfloat16)

    def pack(group, carry):
        at = pl.ds(pl.multiple_of(group * GROUP_ROWS, GROUP_ROWS), GROUP_ROWS)
        pack_group(swap_ref, rows_of, at, out_ref, group * group_block)
        return carry

    lax.fori_loop(0, groups, pack, 0, unroll=4)


def run_expert(arrived, swap, w_in, w_out):
    slots = arrived.shape[0] // PIECES
    any_spec = pl.BlockSpec(memory_space=pl.ANY)
    return pl.pallas_call(
        expert_kernel,
        out_shape=jax.ShapeDtypeStruct(arrived.shape, jnp.bfloat16),
        in_specs=[VMEM_SPEC, VMEM_SPEC, any_spec, any_spec],
        out_specs=VMEM_SPEC,
        scratch_shapes=[
            pltpu.VMEM(w_in.shape, jnp.bfloat16),
            pltpu.VMEM(w_out.shape, jnp.bfloat16),
            pltpu.SemaphoreType.DMA((2, PIECES // STEP_PIECES)),
            pltpu.VMEM((PIECES, slots, PIECE), jnp.bfloat16),
            pltpu.VMEM((slots, 2 * FF), jnp.float32),
            pltpu.VMEM((slots, FF), jnp.bfloat16),
        ],
        compiler_params=pltpu.CompilerParams(vmem_limit_bytes=EXPERT_VMEM),
        name="expert",
    )(arrived, swap, w_in, w_out)


def combine_kernel(target_ref, route_ref, hidden_ref, swap_ref, back_ref, out_ref, rows_of):
    step = pl.program_id(0)
    group_block = GROUP_ROWS * PIECES
    for part in range(STEP_GROUPS):
        to = (step * STEP_GROUPS + part) * GROUP_ROWS
        to = pl.ds(pl.multiple_of(to, GROUP_ROWS), GROUP_ROWS)
        unpack_group(swap_ref, back_ref, part * group_block, rows_of, to)

    @pl.when(step == pl.num_programs(0) - 1)
    def _():
        slots, tokens = rows_of.shape[1], hidden_ref.shape[0]
        route = route_ref[...]
        mixing = route / jnp.sum(route, axis=-1, keepdims=True)
        slot = lax.broadcasted_iota(jnp.int32, (tokens, slots), 1)
        spread = jnp.zeros((tokens, slots), jnp.float32)
        for number in range(TOPK):
            spread += jnp.where(
                slot == target_ref[:, number : number + 1], mixing[:, number : number + 1], 0.0
            )
        high = spread.astype(jnp.bfloat16)
        low = (spread - high.astype(jnp.float32)).astype(jnp.bfloat16)
        both = jnp.concatenate([high, low], 0)
        for piece in range(PIECES):
            columns = slice(piece * PIECE, (piece + 1) * PIECE)
            mixed = dot_f32(both, rows_of[piece])
            out_ref[:, columns] = (
                hidden_ref[:, columns].astype(jnp.float32) + mixed[:tokens] + mixed[tokens:]
            ).astype(jnp.bfloat16)


def combine(target, route_weights, hidden, swap, back):
    tokens, model = hidden.shape
    slots = back.shape[0] // PIECES
    group_block = GROUP_ROWS * PIECES

    def whole(shape):
        return pl.BlockSpec(shape, lambda step: (0, 0))

    return pl.pallas_call(
        combine_kernel,
        grid=(slots // (GROUP_ROWS * STEP_GROUPS),),
        out_shape=jax.ShapeDtypeStruct((tokens, model), jnp.bfloat16),
        in_specs=[
            whole((tokens, TOPK)),
            whole((tokens, TOPK)),
            whole((tokens, model)),
            pl.BlockSpec(swap.shape, lambda step: (0, 0, 0)),
            pl.BlockSpec((STEP_GROUPS * group_block, PIECE), lambda step: (step, 0)),
        ],
        out_specs=whole((tokens, model)),
        scratch_shapes=[pltpu.VMEM((PIECES, slots, PIECE), jnp.bfloat16)],
        compiler_params=pltpu.CompilerParams(vmem_limit_bytes=VMEM_BYTES),
        name="combine",
    )(target, route_weights, hidden, swap, back)


def body(
    queries, keys, values, out_proj, residual, norm_gain, expert_ids, route_weights, w_in, w_out
):
    ctx_count = lax.axis_size("ctx")
    dev_count = ctx_count * lax.axis_size("tp")
    ctx_index = lax.axis_index("ctx")
    heads_here = queries.shape[1] // HEAD_DIM
    kv_index = lax.axis_index("tp") * heads_here // (HEADS // KV_HEADS)
    half = queries.shape[0] // 2

    flat_ids = expert_ids.reshape(-1)
    one_hot = (flat_ids[:, None] == jnp.arange(dev_count, dtype=jnp.int32)[None, :]).astype(
        jnp.int32
    )
    earlier = jnp.cumsum(one_hot, axis=0) - one_hot
    target = (flat_ids * CAP + jnp.sum(earlier * one_hot, axis=1)).reshape(expert_ids.shape)
    swap = piece_swap()

    opposite = [(i, ctx_count - 1 - i) for i in range(ctx_count)]
    swapped = lax.ppermute(queries[half:], "ctx", opposite)
    parity = lax.axis_index("tp") % 2
    place = jnp.stack(
        [2 * ctx_count - 1 - 2 * ctx_index, 2 * ctx_index, parity, kv_index]
    ).astype(jnp.int32)
    mine = lax.all_gather(own_half(place, keys, values, half), "ctx", axis=0, tiled=True)
    swapped, mine = lax.optimization_barrier((swapped, mine))
    other = lax.ppermute(mine, "tp", [(i, i ^ 1) for i in range(lax.axis_size("tp"))])
    full_proj = lax.all_gather(out_proj, "ctx", axis=0, tiled=False)
    far, near = attend(place, swapped, queries[:half], mine, other)
    returned = lax.ppermute(far, "ctx", opposite)
    projected = project(returned, full_proj, 1, project(near, full_proj, 0))
    attn_out = lax.psum_scatter(projected, "tp", scatter_dimension=0, tiled=True)

    hidden, packed = dispatch(
        target.T, attn_out, residual, norm_gain.reshape(1, -1), swap, dev_count
    )

    def exchange(rows):
        shaped = rows.reshape(dev_count, CAP * PIECES, PIECE)
        return lax.all_to_all(
            shaped, ("ctx", "tp"), split_axis=0, concat_axis=0, tiled=True
        ).reshape(rows.shape)

    processed = run_expert(exchange(packed), swap, w_in[0], w_out[0])
    return combine(target, route_weights, hidden, swap, exchange(processed))


def solution(mesh):
    return jax.shard_map(
        body,
        mesh=mesh,
        in_specs=(
            P("ctx", "tp"),
            P("ctx", None),
            P("ctx", None),
            P("tp", "ctx"),
            P(("ctx", "tp"), None),
            P(),
            P(("ctx", "tp"), None),
            P(("ctx", "tp"), None),
            P(("ctx", "tp"), None, None),
            P(("ctx", "tp"), None, None),
        ),
        out_specs=P(("ctx", "tp"), None),
        check_vma=False,
    )
```

```python
import functools
import math

import jax
import jax.numpy as jnp
import numpy as np
from jax import lax
from jax.experimental import pallas as pl
from jax.experimental.pallas import tpu as pltpu
from jax.sharding import PartitionSpec as P

HEADS = 32
KV_HEADS = 2
HEAD_DIM = 128
FF = 768
TOPK = 4
CAP = 6
BASE2_SCALE = math.log2(math.e) / math.sqrt(HEAD_DIM)
EXPONENT_LIMIT = 100.0
KEY_WIDTH = 1024
SUB_ROWS = 512
WIDE_ROWS = 2048
PIECE = 512
PIECES = 8
GROUP = 8
GROUP_ROWS = GROUP * CAP
STEP_GROUPS = 4
STEP_PIECES = 2
PROJECT_WIDTH = 1024
VMEM_BYTES = 56 * 2**20
EXPERT_VMEM = 46 * 2**20
ATTEND_VMEM = 36 * 2**20

VMEM_SPEC = pl.BlockSpec(memory_space=pltpu.VMEM)
SMEM_SPEC = pl.BlockSpec(memory_space=pltpu.SMEM)


def piece_swap():
    devices = GROUP // 2
    swap = np.zeros((PIECES, devices, CAP, devices, PIECES, CAP), np.float32)
    for device in range(devices):
        for piece in range(PIECES):
            for slot in range(CAP):
                swap[piece, device, slot, device, piece, slot] = 1
    size = devices * PIECES * CAP
    swap = swap.reshape(size, size)
    return jnp.asarray(np.stack([swap, swap.T]), jnp.bfloat16)


def unpack_group(swap_ref, message_ref, first, rows_of, to):
    size = swap_ref.shape[1]
    part = size // PIECES
    halves = [
        dot_f32(swap_ref[0], message_ref[pl.ds(pl.multiple_of(first + half * size, size), size), :])
        for half in range(2)
    ]
    for piece in range(PIECES):
        rows_of[piece, to, :] = jnp.concatenate(
            [half[piece * part : (piece + 1) * part] for half in halves], 0
        ).astype(jnp.bfloat16)


def pack_group(swap_ref, rows_of, at, message_ref, first, second=None):
    size = swap_ref.shape[1]
    part = size // PIECES
    pieces = [rows_of[piece, at, :].astype(jnp.float32) for piece in range(PIECES)]
    for half in range(2):
        stacked = jnp.concatenate([rows[half * part : (half + 1) * part] for rows in pieces], 0)
        to = first + half * size if second is None or half == 0 else second
        message_ref[pl.ds(pl.multiple_of(to, size), size), :] = dot_f32(
            swap_ref[1], stacked.astype(jnp.bfloat16)
        ).astype(jnp.bfloat16)


def dot_f32(left, right):
    return jnp.dot(left, right, preferred_element_type=jnp.float32)


def dot_keys(left, keys):
    return lax.dot_general(
        left, keys, (((1,), (1,)), ((), ())), preferred_element_type=jnp.float32
    )


def own_half_kernel(place_ref, keys_ref, values_ref, out_ref):
    out_ref[:, :HEAD_DIM] = keys_ref[...]
    out_ref[:, HEAD_DIM:] = values_ref[...]


def own_half(place, keys, values, half):
    taken = pl.BlockSpec((half, HEAD_DIM), lambda step, place_ref: (place_ref[2], place_ref[3]))
    return pl.pallas_call(
        own_half_kernel,
        grid_spec=pltpu.PrefetchScalarGridSpec(
            num_scalar_prefetch=1,
            grid=(1,),
            in_specs=[taken, taken],
            out_specs=pl.BlockSpec((half, 2 * HEAD_DIM), lambda step, place_ref: (0, 0)),
        ),
        out_shape=jax.ShapeDtypeStruct((half, 2 * HEAD_DIM), jnp.bfloat16),
        name="own_half",
    )(place, keys, values)


def attend_part(block, shift, parity, q_ref, mine_ref, other_ref, out_ref, q_wide, top, acc):
    rows, width, sub = q_ref.shape[0], KEY_WIDTH, SUB_ROWS
    heads = q_ref.shape[1] // HEAD_DIM
    tiles = heads * rows // sub
    last = (block * rows) // width
    bound = jnp.full((1, 1), jnp.inf, jnp.float32)
    ones = jnp.ones((acc.shape[0] - HEAD_DIM, width), jnp.bfloat16)

    def load(index, ordered=False):
        at = pl.ds(pl.multiple_of(index * (width // 2), width // 2), width // 2)
        first, second = mine_ref[at, :], other_ref[at, :]
        if ordered:
            swapped = parity > 0
            first, second = jnp.where(swapped, second, first), jnp.where(swapped, first, second)
        both = jnp.concatenate([first, second], 0)
        keys, values = both[:, :HEAD_DIM], both[:, HEAD_DIM:]
        return jnp.concatenate([keys, keys], 1), jnp.concatenate([values.T, ones], 0)

    norms = []
    for head in range(heads):
        scaled = q_ref[:, head * HEAD_DIM : (head + 1) * HEAD_DIM].astype(jnp.float32) * BASE2_SCALE
        high = scaled.astype(jnp.bfloat16)
        q_wide[head * rows : (head + 1) * rows, :HEAD_DIM] = high
        q_wide[head * rows : (head + 1) * rows, HEAD_DIM:] = (
            scaled - high.astype(jnp.float32)
        ).astype(jnp.bfloat16)
        norms.append(jnp.max(jnp.sum(scaled * scaled, axis=1, keepdims=True), axis=0, keepdims=True))
    longest_query = jnp.sqrt(functools.reduce(jnp.maximum, norms))

    keys, values = load(last, ordered=True)
    least = jnp.full((1, sub), jnp.inf, jnp.float32)
    for tile in range(tiles):
        at = slice(tile * sub, (tile + 1) * sub)
        first = (tile * sub) % rows
        seen = shift + first + sub
        scores = dot_keys(keys[:seen], q_wide[at, :])
        key = lax.broadcasted_iota(jnp.int32, (seen, sub), 0)
        row = lax.broadcasted_iota(jnp.int32, (seen, sub), 1) + (first + shift)
        scores = jnp.where(key <= row, scores, -1e30)
        best = jnp.max(scores, axis=0, keepdims=True)
        weights = jnp.exp2(scores - best).astype(jnp.bfloat16)
        acc[:, at] = dot_f32(values[:, :seen], weights)
        top[:, at] = jnp.broadcast_to(best, (top.shape[0], sub))
        least = jnp.minimum(least, best)
    bound = (EXPONENT_LIMIT + jnp.min(least, axis=1, keepdims=True)) / longest_query

    def longest(index, so_far):
        at = pl.ds(pl.multiple_of(index * (width // 2), width // 2), width // 2)
        for held in (mine_ref, other_ref):
            keys = held[at, :HEAD_DIM].astype(jnp.float32)
            length = jnp.sum(keys * keys, axis=1, keepdims=True)
            so_far = jnp.maximum(so_far, jnp.max(length, axis=0, keepdims=True))
        return so_far

    key_norm = jnp.sqrt(lax.fori_loop(0, last, longest, jnp.zeros((1, 1), jnp.float32)))
    safe = jnp.max(key_norm - bound) <= 0.0

    @pl.when(safe)
    def _():
        def step(index, carry):
            keys, values = load(index)
            for first in range(0, heads * rows, WIDE_ROWS):
                at = slice(first, first + WIDE_ROWS)
                scores = dot_keys(keys, q_wide[at, :])
                weights = jnp.exp2(scores - top[:1, at]).astype(jnp.bfloat16)
                acc[:, at] += dot_f32(values, weights)
            return carry

        lax.fori_loop(0, last, step, 0)

    @pl.when(jnp.logical_not(safe))
    def _():
        def step(index, carry):
            keys, values = load(index)
            for tile in range(tiles):
                at = slice(tile * sub, (tile + 1) * sub)
                scores = dot_keys(keys, q_wide[at, :])
                old = top[:1, at]
                best = jnp.maximum(old, jnp.max(scores, axis=0, keepdims=True))
                weights = jnp.exp2(scores - best).astype(jnp.bfloat16)
                acc[:, at] = acc[:, at] * jnp.exp2(old - best) + dot_f32(values, weights)
                top[:, at] = jnp.broadcast_to(best, (top.shape[0], sub))
            return carry

        lax.fori_loop(0, last, step, 0)

    for head in range(heads):
        at = slice(head * rows, (head + 1) * rows)
        mean = acc[:HEAD_DIM, at] / acc[HEAD_DIM : HEAD_DIM + 1, at]
        out_ref[:, head * HEAD_DIM : (head + 1) * HEAD_DIM] = mean.T.astype(jnp.bfloat16)


def attend_kernel(place_ref, far_ref, near_ref, mine_ref, other_ref, out_ref, *scratch):
    rows = near_ref.shape[0]
    near_out, far_out = out_ref.at[pl.ds(0, rows), :], out_ref.at[pl.ds(rows, rows), :]
    parity = place_ref[2]
    attend_part(place_ref[0], rows, parity, far_ref, mine_ref, other_ref, far_out, *scratch)
    attend_part(place_ref[1], 0, parity, near_ref, mine_ref, other_ref, near_out, *scratch)


def attend(place, far, near, mine, other):
    rows, columns = near.shape
    all_rows = rows * columns // HEAD_DIM
    return pl.pallas_call(
        attend_kernel,
        out_shape=jax.ShapeDtypeStruct((2 * rows, columns), jnp.bfloat16),
        in_specs=[SMEM_SPEC] + [VMEM_SPEC] * 4,
        out_specs=VMEM_SPEC,
        scratch_shapes=[
            pltpu.VMEM((all_rows, 2 * HEAD_DIM), jnp.bfloat16),
            pltpu.VMEM((8, all_rows), jnp.float32),
            pltpu.VMEM((HEAD_DIM + 16, all_rows), jnp.float32),
        ],
        compiler_params=pltpu.CompilerParams(vmem_limit_bytes=ATTEND_VMEM),
        name="attend",
    )(place, far, near, mine, other)


def project_kernel(attended_ref, proj_ref, out_ref):
    proj = jnp.concatenate([proj_ref[part] for part in range(proj_ref.shape[0])], 1)
    out_ref[...] = dot_f32(attended_ref[...], proj).astype(jnp.bfloat16)


def project(attended, proj):
    rows, depth = attended.shape
    parts, _, width = proj.shape
    taken = PROJECT_WIDTH // width
    return pl.pallas_call(
        project_kernel,
        grid=(parts // taken,),
        out_shape=jax.ShapeDtypeStruct((rows, parts * width), jnp.bfloat16),
        in_specs=[
            pl.BlockSpec((rows, depth), lambda step: (0, 0)),
            pl.BlockSpec((taken, depth, width), lambda step: (step, 0, 0)),
        ],
        out_specs=pl.BlockSpec((rows, taken * width), lambda step: (0, step)),
        compiler_params=pltpu.CompilerParams(vmem_limit_bytes=VMEM_BYTES),
        name="project",
    )(attended, proj)


def dispatch_kernel(target_ref, attn_ref, residual_ref, gain_ref, swap_ref, hidden_ref, out_ref, rows_of):
    step = pl.program_id(0)

    @pl.when(step == 0)
    def _():
        hidden = (
            residual_ref[...].astype(jnp.float32) + attn_ref[...].astype(jnp.float32)
        ).astype(jnp.bfloat16)
        hidden_ref[...] = hidden
        wide = hidden.astype(jnp.float32)
        variance = jnp.mean(wide * wide, axis=-1, keepdims=True)
        normed = (wide * lax.rsqrt(variance + 1e-06) * gain_ref[...]).astype(jnp.bfloat16)
        slots, tokens = rows_of.shape[1], normed.shape[0]
        slot = lax.broadcasted_iota(jnp.int32, (slots, tokens), 0)
        chosen = jnp.zeros((slots, tokens), jnp.float32)
        for route in range(TOPK):
            chosen += jnp.where(slot == target_ref[route : route + 1, :], 1.0, 0.0)
        chosen = chosen.astype(jnp.bfloat16)
        for piece in range(PIECES):
            rows_of[piece] = dot_f32(
                chosen, normed[:, piece * PIECE : (piece + 1) * PIECE]
            ).astype(jnp.bfloat16)

    group_block = GROUP_ROWS * PIECES
    for part in range(STEP_GROUPS):
        at = (step * STEP_GROUPS + part) * GROUP_ROWS
        at = pl.ds(pl.multiple_of(at, GROUP_ROWS), GROUP_ROWS)
        pack_group(swap_ref, rows_of, at, out_ref, part * group_block)


def dispatch(target, attn_out, residual, gain, swap, dev_count):
    tokens, model = residual.shape
    slots = dev_count * CAP
    group_block = GROUP_ROWS * PIECES

    def whole(shape):
        return pl.BlockSpec(shape, lambda step: (0, 0))

    return pl.pallas_call(
        dispatch_kernel,
        grid=(dev_count // (GROUP * STEP_GROUPS),),
        out_shape=(
            jax.ShapeDtypeStruct((tokens, model), jnp.bfloat16),
            jax.ShapeDtypeStruct((slots * PIECES, PIECE), jnp.bfloat16),
        ),
        in_specs=[
            whole((TOPK, tokens)),
            whole((tokens, model)),
            whole((tokens, model)),
            whole((1, model)),
            pl.BlockSpec(swap.shape, lambda step: (0, 0, 0)),
        ],
        out_specs=(
            whole((tokens, model)),
            pl.BlockSpec((STEP_GROUPS * group_block, PIECE), lambda step: (step, 0)),
        ),
        scratch_shapes=[pltpu.VMEM((PIECES, slots, PIECE), jnp.bfloat16)],
        compiler_params=pltpu.CompilerParams(vmem_limit_bytes=VMEM_BYTES),
        name="norm_and_dispatch",
    )(target, attn_out, residual, gain, swap)


def expert_kernel(
    arrived_ref, swap_ref, in_hbm, down_hbm, out_ref, in_ref, down_ref, landed, rows_of, gate_up, active
):
    groups = rows_of.shape[1] // GROUP_ROWS
    group_block = GROUP_ROWS * PIECES
    steps = PIECES // STEP_PIECES
    width = STEP_PIECES * PIECE

    def columns(step):
        return slice(step * width, (step + 1) * width)

    weights_in = [
        pltpu.make_async_copy(in_hbm.at[columns(step), :], in_ref.at[columns(step), :], landed.at[0, step])
        for step in range(steps)
    ]
    weights_down = [
        pltpu.make_async_copy(
            down_hbm.at[:, columns(step)], down_ref.at[:, columns(step)], landed.at[1, step]
        )
        for step in range(steps)
    ]
    for copy in weights_in + weights_down:
        copy.start()

    def unpack(group, carry):
        to = pl.ds(pl.multiple_of(group * GROUP_ROWS, GROUP_ROWS), GROUP_ROWS)
        unpack_group(swap_ref, arrived_ref, group * group_block, rows_of, to)
        return carry

    lax.fori_loop(0, groups, unpack, 0, unroll=4)
    for step in range(steps):
        weights_in[step].wait()
        pieces = range(step * STEP_PIECES, (step + 1) * STEP_PIECES)
        rows = jnp.concatenate([rows_of[piece] for piece in pieces], 1)
        part = dot_f32(rows, in_ref[columns(step), :])
        if step == 0:
            gate_up[...] = part
        else:
            gate_up[...] += part
    active[...] = (jax.nn.silu(gate_up[:, :FF]) * gate_up[:, FF:]).astype(jnp.bfloat16)
    for step in range(steps):
        weights_down[step].wait()
        for piece in range(step * STEP_PIECES, (step + 1) * STEP_PIECES):
            rows_of[piece] = dot_f32(
                active[...], down_ref[:, piece * PIECE : (piece + 1) * PIECE]
            ).astype(jnp.bfloat16)

    def pack(group, carry):
        at = pl.ds(pl.multiple_of(group * GROUP_ROWS, GROUP_ROWS), GROUP_ROWS)
        second = (groups - 1 - group) * group_block + group_block // 2
        pack_group(swap_ref, rows_of, at, out_ref, group * group_block, second)
        return carry

    lax.fori_loop(0, groups, pack, 0, unroll=4)


def run_expert(arrived, swap, w_in, w_out):
    slots = arrived.shape[0] // PIECES
    any_spec = pl.BlockSpec(memory_space=pl.ANY)
    return pl.pallas_call(
        expert_kernel,
        out_shape=jax.ShapeDtypeStruct(arrived.shape, jnp.bfloat16),
        in_specs=[VMEM_SPEC, VMEM_SPEC, any_spec, any_spec],
        out_specs=VMEM_SPEC,
        scratch_shapes=[
            pltpu.VMEM(w_in.shape, jnp.bfloat16),
            pltpu.VMEM(w_out.shape, jnp.bfloat16),
            pltpu.SemaphoreType.DMA((2, PIECES // STEP_PIECES)),
            pltpu.VMEM((PIECES, slots, PIECE), jnp.bfloat16),
            pltpu.VMEM((slots, 2 * FF), jnp.float32),
            pltpu.VMEM((slots, FF), jnp.bfloat16),
        ],
        compiler_params=pltpu.CompilerParams(vmem_limit_bytes=EXPERT_VMEM),
        name="expert",
    )(arrived, swap, w_in, w_out)


def combine_kernel(target_ref, route_ref, hidden_ref, swap_ref, back_ref, out_ref, rows_of):
    step = pl.program_id(0)
    group_block = GROUP_ROWS * PIECES
    for part in range(STEP_GROUPS):
        to = (step * STEP_GROUPS + part) * GROUP_ROWS
        to = pl.ds(pl.multiple_of(to, GROUP_ROWS), GROUP_ROWS)
        unpack_group(swap_ref, back_ref, part * group_block, rows_of, to)

    @pl.when(step == pl.num_programs(0) - 1)
    def _():
        slots, tokens = rows_of.shape[1], hidden_ref.shape[0]
        route = route_ref[...]
        mixing = route / jnp.sum(route, axis=-1, keepdims=True)
        slot = lax.broadcasted_iota(jnp.int32, (tokens, slots), 1)
        spread = jnp.zeros((tokens, slots), jnp.float32)
        for number in range(TOPK):
            spread += jnp.where(
                slot == target_ref[:, number : number + 1], mixing[:, number : number + 1], 0.0
            )
        high = spread.astype(jnp.bfloat16)
        low = (spread - high.astype(jnp.float32)).astype(jnp.bfloat16)
        both = jnp.concatenate([high, low], 0)
        for piece in range(PIECES):
            columns = slice(piece * PIECE, (piece + 1) * PIECE)
            mixed = dot_f32(both, rows_of[piece])
            out_ref[:, columns] = (
                hidden_ref[:, columns].astype(jnp.float32) + mixed[:tokens] + mixed[tokens:]
            ).astype(jnp.bfloat16)


def combine(target, route_weights, hidden, swap, back):
    tokens, model = hidden.shape
    slots = back.shape[0] // PIECES
    group_block = GROUP_ROWS * PIECES

    def whole(shape):
        return pl.BlockSpec(shape, lambda step: (0, 0))

    return pl.pallas_call(
        combine_kernel,
        grid=(slots // (GROUP_ROWS * STEP_GROUPS),),
        out_shape=jax.ShapeDtypeStruct((tokens, model), jnp.bfloat16),
        in_specs=[
            whole((tokens, TOPK)),
            whole((tokens, TOPK)),
            whole((tokens, model)),
            pl.BlockSpec(swap.shape, lambda step: (0, 0, 0)),
            pl.BlockSpec((STEP_GROUPS * group_block, PIECE), lambda step: (step, 0)),
        ],
        out_specs=whole((tokens, model)),
        scratch_shapes=[pltpu.VMEM((PIECES, slots, PIECE), jnp.bfloat16)],
        compiler_params=pltpu.CompilerParams(vmem_limit_bytes=VMEM_BYTES),
        name="combine",
    )(target, route_weights, hidden, swap, back)


def body(
    queries, keys, values, out_proj, residual, norm_gain, expert_ids, route_weights, w_in, w_out
):
    ctx_count = lax.axis_size("ctx")
    dev_count = ctx_count * lax.axis_size("tp")
    ctx_index = lax.axis_index("ctx")
    heads_here = queries.shape[1] // HEAD_DIM
    kv_index = lax.axis_index("tp") * heads_here // (HEADS // KV_HEADS)
    half = queries.shape[0] // 2

    flat_ids = expert_ids.reshape(-1)
    one_hot = (flat_ids[:, None] == jnp.arange(dev_count, dtype=jnp.int32)[None, :]).astype(
        jnp.int32
    )
    earlier = jnp.cumsum(one_hot, axis=0) - one_hot
    target = (flat_ids * CAP + jnp.sum(earlier * one_hot, axis=1)).reshape(expert_ids.shape)
    swap = piece_swap()

    opposite = [(i, ctx_count - 1 - i) for i in range(ctx_count)]
    swapped = lax.ppermute(queries[half:], "ctx", opposite)
    parity = lax.axis_index("tp") % 2
    place = jnp.stack(
        [2 * ctx_count - 1 - 2 * ctx_index, 2 * ctx_index, parity, kv_index]
    ).astype(jnp.int32)
    mine = lax.all_gather(own_half(place, keys, values, half), "ctx", axis=0, tiled=True)
    swapped, mine = lax.optimization_barrier((swapped, mine))
    other = lax.ppermute(mine, "tp", [(i, i ^ 1) for i in range(lax.axis_size("tp"))])
    full_proj = lax.all_gather(out_proj, "ctx", axis=0, tiled=False)
    projected = project(attend(place, swapped, queries[:half], mine, other), full_proj)
    attn_out = lax.psum_scatter(projected, "tp", scatter_dimension=0, tiled=True)

    tp_count = dev_count // ctx_count
    home = [
        (c * tp_count + t, (c if 2 * t < tp_count else ctx_count - 1 - c) * tp_count + t)
        for c in range(ctx_count)
        for t in range(tp_count)
    ]

    def trade(array):
        return lax.ppermute(array, ("ctx", "tp"), home)

    residual, projected = lax.optimization_barrier((residual, projected))
    hidden, packed = dispatch(
        trade(target).T, attn_out, trade(residual), norm_gain.reshape(1, -1), swap, dev_count
    )

    def exchange(rows):
        shaped = rows.reshape(dev_count, CAP * PIECES, PIECE)
        return lax.all_to_all(
            shaped, ("ctx", "tp"), split_axis=0, concat_axis=0, tiled=True
        ).reshape(rows.shape)

    hidden, arrived = lax.optimization_barrier((hidden, exchange(packed)))
    processed = run_expert(arrived, swap, w_in[0], w_out[0])
    return combine(target, route_weights, trade(hidden), swap, exchange(processed))


def solution(mesh):
    return jax.shard_map(
        body,
        mesh=mesh,
        in_specs=(
            P("ctx", "tp"),
            P("ctx", None),
            P("ctx", None),
            P("tp", "ctx"),
            P(("ctx", "tp"), None),
            P(),
            P(("ctx", "tp"), None),
            P(("ctx", "tp"), None),
            P(("ctx", "tp"), None, None),
            P(("ctx", "tp"), None, None),
        ),
        out_specs=P(("ctx", "tp"), None),
        check_vma=False,
    )
```

```python
import functools
import math

import jax
import jax.numpy as jnp
import numpy as np
from jax import lax
from jax.experimental import pallas as pl
from jax.experimental.pallas import tpu as pltpu
from jax.sharding import PartitionSpec as P

HEADS = 32
KV_HEADS = 2
HEAD_DIM = 128
FF = 768
TOPK = 4
CAP = 6
BASE2_SCALE = math.log2(math.e) / math.sqrt(HEAD_DIM)
EXPONENT_LIMIT = 100.0
KEY_WIDTH = 1024
SUB_ROWS = 512
WIDE_ROWS = 2048
PIECE = 512
PIECES = 8
GROUP = 8
GROUP_ROWS = GROUP * CAP
DISPATCH_GROUPS = 8
STEP_GROUPS = 4
STEP_PIECES = 2
PROJECT_WIDTH = 1024
VMEM_BYTES = 56 * 2**20
EXPERT_VMEM = 46 * 2**20
ATTEND_VMEM = 36 * 2**20

VMEM_SPEC = pl.BlockSpec(memory_space=pltpu.VMEM)
SMEM_SPEC = pl.BlockSpec(memory_space=pltpu.SMEM)


def piece_swap():
    devices = GROUP // 2
    length = PIECES * CAP
    swap = np.zeros((3, devices * length, devices * length), np.float32)
    for device in range(devices):
        for piece in range(PIECES):
            for slot in range(CAP):
                to = (piece * devices + device) * CAP + slot
                swap[0, to, device * length + piece * CAP + slot] = 1
                swap[2, to, device * length + tile_row(piece, slot)] = 1
    swap[1] = swap[0].T
    return jnp.asarray(swap, jnp.bfloat16)


def tile_row(piece, slot):
    if piece < CAP:
        return piece * 8 + slot
    return ((piece - CAP) * (CAP // 2) + slot // 2) * 8 + CAP + slot % 2


def unpack_group(swap_ref, which, message_ref, first, rows_of, to):
    size = swap_ref.shape[1]
    part = size // PIECES
    halves = [
        dot_f32(swap_ref[which], message_ref[pl.ds(pl.multiple_of(first + half * size, size), size), :])
        for half in range(2)
    ]
    for piece in range(PIECES):
        rows_of[piece, to, :] = jnp.concatenate(
            [half[piece * part : (piece + 1) * part] for half in halves], 0
        ).astype(jnp.bfloat16)


def pack_group(swap_ref, rows_of, at, message_ref, first, second=None):
    size = swap_ref.shape[1]
    part = size // PIECES
    pieces = [rows_of[piece, at, :].astype(jnp.float32) for piece in range(PIECES)]
    for half in range(2):
        stacked = jnp.concatenate([rows[half * part : (half + 1) * part] for rows in pieces], 0)
        to = first + half * size if second is None or half == 0 else second
        message_ref[pl.ds(pl.multiple_of(to, size), size), :] = dot_f32(
            swap_ref[1], stacked.astype(jnp.bfloat16)
        ).astype(jnp.bfloat16)


def dot_f32(left, right):
    return jnp.dot(left, right, preferred_element_type=jnp.float32)


def dot_keys(left, keys):
    return lax.dot_general(
        left, keys, (((1,), (1,)), ((), ())), preferred_element_type=jnp.float32
    )


def own_half_kernel(place_ref, keys_ref, values_ref, out_ref):
    out_ref[:, :HEAD_DIM] = keys_ref[...]
    out_ref[:, HEAD_DIM:] = values_ref[...]


def own_half(place, keys, values, half):
    taken = pl.BlockSpec((half, HEAD_DIM), lambda step, place_ref: (place_ref[2], place_ref[3]))
    return pl.pallas_call(
        own_half_kernel,
        grid_spec=pltpu.PrefetchScalarGridSpec(
            num_scalar_prefetch=1,
            grid=(1,),
            in_specs=[taken, taken],
            out_specs=pl.BlockSpec((half, 2 * HEAD_DIM), lambda step, place_ref: (0, 0)),
        ),
        out_shape=jax.ShapeDtypeStruct((half, 2 * HEAD_DIM), jnp.bfloat16),
        name="own_half",
    )(place, keys, values)


def attend_part(block, shift, parity, q_ref, mine_ref, other_ref, out_ref, q_wide, top, acc):
    rows, width, sub = q_ref.shape[0], KEY_WIDTH, SUB_ROWS
    heads = q_ref.shape[1] // HEAD_DIM
    tiles = heads * rows // sub
    last = (block * rows) // width
    bound = jnp.full((1, 1), jnp.inf, jnp.float32)
    ones = jnp.ones((acc.shape[0] - HEAD_DIM, width), jnp.bfloat16)

    def load(index, ordered=False):
        at = pl.ds(pl.multiple_of(index * (width // 2), width // 2), width // 2)
        first, second = mine_ref[at, :], other_ref[at, :]
        if ordered:
            swapped = parity > 0
            first, second = jnp.where(swapped, second, first), jnp.where(swapped, first, second)
        both = jnp.concatenate([first, second], 0)
        keys, values = both[:, :HEAD_DIM], both[:, HEAD_DIM:]
        return jnp.concatenate([keys, keys], 1), jnp.concatenate([values.T, ones], 0)

    norms = []
    for head in range(heads):
        scaled = q_ref[:, head * HEAD_DIM : (head + 1) * HEAD_DIM].astype(jnp.float32) * BASE2_SCALE
        high = scaled.astype(jnp.bfloat16)
        q_wide[head * rows : (head + 1) * rows, :HEAD_DIM] = high
        q_wide[head * rows : (head + 1) * rows, HEAD_DIM:] = (
            scaled - high.astype(jnp.float32)
        ).astype(jnp.bfloat16)
        norms.append(jnp.max(jnp.sum(scaled * scaled, axis=1, keepdims=True), axis=0, keepdims=True))
    longest_query = jnp.sqrt(functools.reduce(jnp.maximum, norms))

    keys, values = load(last, ordered=True)
    least = jnp.full((1, sub), jnp.inf, jnp.float32)
    for tile in range(tiles):
        at = slice(tile * sub, (tile + 1) * sub)
        first = (tile * sub) % rows
        seen = shift + first + sub
        scores = dot_keys(keys[:seen], q_wide[at, :])
        key = lax.broadcasted_iota(jnp.int32, (seen, sub), 0)
        row = lax.broadcasted_iota(jnp.int32, (seen, sub), 1) + (first + shift)
        scores = jnp.where(key <= row, scores, -1e30)
        best = jnp.max(scores, axis=0, keepdims=True)
        weights = jnp.exp2(scores - best).astype(jnp.bfloat16)
        acc[:, at] = dot_f32(values[:, :seen], weights)
        top[:, at] = jnp.broadcast_to(best, (top.shape[0], sub))
        least = jnp.minimum(least, best)
    bound = (EXPONENT_LIMIT + jnp.min(least, axis=1, keepdims=True)) / longest_query

    def longest(index, so_far):
        at = pl.ds(pl.multiple_of(index * (width // 2), width // 2), width // 2)
        for held in (mine_ref, other_ref):
            keys = held[at, :HEAD_DIM].astype(jnp.float32)
            length = jnp.sum(keys * keys, axis=1, keepdims=True)
            so_far = jnp.maximum(so_far, jnp.max(length, axis=0, keepdims=True))
        return so_far

    key_norm = jnp.sqrt(lax.fori_loop(0, last, longest, jnp.zeros((1, 1), jnp.float32)))
    safe = jnp.max(key_norm - bound) <= 0.0

    @pl.when(safe)
    def _():
        def step(index, carry):
            keys, values = load(index)
            for first in range(0, heads * rows, WIDE_ROWS):
                at = slice(first, first + WIDE_ROWS)
                scores = dot_keys(keys, q_wide[at, :])
                weights = jnp.exp2(scores - top[:1, at]).astype(jnp.bfloat16)
                acc[:, at] += dot_f32(values, weights)
            return carry

        lax.fori_loop(0, last, step, 0)

    @pl.when(jnp.logical_not(safe))
    def _():
        def step(index, carry):
            keys, values = load(index)
            for tile in range(tiles):
                at = slice(tile * sub, (tile + 1) * sub)
                scores = dot_keys(keys, q_wide[at, :])
                old = top[:1, at]
                best = jnp.maximum(old, jnp.max(scores, axis=0, keepdims=True))
                weights = jnp.exp2(scores - best).astype(jnp.bfloat16)
                acc[:, at] = acc[:, at] * jnp.exp2(old - best) + dot_f32(values, weights)
                top[:, at] = jnp.broadcast_to(best, (top.shape[0], sub))
            return carry

        lax.fori_loop(0, last, step, 0)

    for head in range(heads):
        at = slice(head * rows, (head + 1) * rows)
        mean = acc[:HEAD_DIM, at] / acc[HEAD_DIM : HEAD_DIM + 1, at]
        out_ref[:, head * HEAD_DIM : (head + 1) * HEAD_DIM] = mean.T.astype(jnp.bfloat16)


def attend_kernel(place_ref, far_ref, near_ref, mine_ref, other_ref, out_ref, *scratch):
    rows = near_ref.shape[0]
    near_out, far_out = out_ref.at[pl.ds(0, rows), :], out_ref.at[pl.ds(rows, rows), :]
    parity = place_ref[2]
    attend_part(place_ref[0], rows, parity, far_ref, mine_ref, other_ref, far_out, *scratch)
    attend_part(place_ref[1], 0, parity, near_ref, mine_ref, other_ref, near_out, *scratch)


def attend(place, far, near, mine, other):
    rows, columns = near.shape
    all_rows = rows * columns // HEAD_DIM
    return pl.pallas_call(
        attend_kernel,
        out_shape=jax.ShapeDtypeStruct((2 * rows, columns), jnp.bfloat16),
        in_specs=[SMEM_SPEC] + [VMEM_SPEC] * 4,
        out_specs=VMEM_SPEC,
        scratch_shapes=[
            pltpu.VMEM((all_rows, 2 * HEAD_DIM), jnp.bfloat16),
            pltpu.VMEM((8, all_rows), jnp.float32),
            pltpu.VMEM((HEAD_DIM + 16, all_rows), jnp.float32),
        ],
        compiler_params=pltpu.CompilerParams(vmem_limit_bytes=ATTEND_VMEM),
        name="attend",
    )(place, far, near, mine, other)


def project_kernel(attended_ref, proj_ref, out_ref):
    proj = jnp.concatenate([proj_ref[part] for part in range(proj_ref.shape[0])], 1)
    out_ref[...] = dot_f32(attended_ref[...], proj).astype(jnp.bfloat16)


def project(attended, proj):
    rows, depth = attended.shape
    parts, _, width = proj.shape
    taken = PROJECT_WIDTH // width
    return pl.pallas_call(
        project_kernel,
        grid=(parts // taken,),
        out_shape=jax.ShapeDtypeStruct((rows, parts * width), jnp.bfloat16),
        in_specs=[
            pl.BlockSpec((rows, depth), lambda step: (0, 0)),
            pl.BlockSpec((taken, depth, width), lambda step: (step, 0, 0)),
        ],
        out_specs=pl.BlockSpec((rows, taken * width), lambda step: (0, step)),
        compiler_params=pltpu.CompilerParams(vmem_limit_bytes=VMEM_BYTES),
        name="project",
    )(attended, proj)


def dispatch_kernel(target_ref, attn_ref, residual_ref, gain_ref, hidden_ref, out_ref, normed):
    step = pl.program_id(0)
    tokens = attn_ref.shape[0]
    devices = out_ref.shape[0]

    @pl.when(step == 0)
    def _():
        hidden = (
            residual_ref[...].astype(jnp.float32) + attn_ref[...].astype(jnp.float32)
        ).astype(jnp.bfloat16)
        hidden_ref[...] = hidden
        wide = hidden.astype(jnp.float32)
        variance = jnp.mean(wide * wide, axis=-1, keepdims=True)
        normed[...] = (wide * lax.rsqrt(variance + 1e-06) * gain_ref[...]).astype(jnp.bfloat16)

    number = lax.broadcasted_iota(jnp.int32, (devices * 8, tokens), 0)
    row = number & 7
    first = (step * devices + (number >> 3)) * CAP

    def chosen(slot):
        found = jnp.zeros(slot.shape, jnp.float32)
        for route in range(TOPK):
            found += jnp.where(slot == target_ref[route : route + 1, :], 1.0, 0.0)
        return found.astype(jnp.bfloat16)

    def columns(piece):
        return normed[:, piece * PIECE : (piece + 1) * PIECE]

    main = chosen(jnp.where(row < CAP, first + row, -1))
    tails = [
        chosen(jnp.where(row >= CAP, first + row - CAP + 2 * pair, -1)) for pair in range(CAP // 2)
    ]
    for pair in range(CAP // 2):
        tiles = []
        for tile in (2 * pair, 2 * pair + 1):
            taken = jnp.concatenate([main, tails[tile % (CAP // 2)]], 1)
            source = jnp.concatenate([columns(tile), columns(CAP + tile // (CAP // 2))], 0)
            tiles.append(dot_f32(taken, source).reshape(devices, 8, PIECE))
        out_ref[:, pair * 16 : (pair + 1) * 16, :] = jnp.concatenate(tiles, 1).astype(jnp.bfloat16)


def dispatch(target, attn_out, residual, gain, dev_count):
    tokens, model = residual.shape
    devices = GROUP * DISPATCH_GROUPS

    def whole(shape):
        return pl.BlockSpec(shape, lambda step: (0, 0))

    return pl.pallas_call(
        dispatch_kernel,
        grid=(dev_count // devices,),
        out_shape=(
            jax.ShapeDtypeStruct((tokens, model), jnp.bfloat16),
            jax.ShapeDtypeStruct((dev_count, CAP * PIECES, PIECE), jnp.bfloat16),
        ),
        in_specs=[
            whole((TOPK, tokens)),
            whole((tokens, model)),
            whole((tokens, model)),
            whole((1, model)),
        ],
        out_specs=(
            whole((tokens, model)),
            pl.BlockSpec((devices, CAP * PIECES, PIECE), lambda step: (step, 0, 0)),
        ),
        scratch_shapes=[pltpu.VMEM((tokens, model), jnp.bfloat16)],
        compiler_params=pltpu.CompilerParams(vmem_limit_bytes=VMEM_BYTES),
        name="norm_and_dispatch",
    )(target, attn_out, residual, gain)


def expert_kernel(
    arrived_ref, swap_ref, in_hbm, down_hbm, out_ref, in_ref, down_ref, landed, rows_of, gate_up, active
):
    groups = rows_of.shape[1] // GROUP_ROWS
    group_block = GROUP_ROWS * PIECES
    steps = PIECES // STEP_PIECES
    width = STEP_PIECES * PIECE

    def columns(step):
        return slice(step * width, (step + 1) * width)

    weights_in = [
        pltpu.make_async_copy(in_hbm.at[columns(step), :], in_ref.at[columns(step), :], landed.at[0, step])
        for step in range(steps)
    ]
    weights_down = [
        pltpu.make_async_copy(
            down_hbm.at[:, columns(step)], down_ref.at[:, columns(step)], landed.at[1, step]
        )
        for step in range(steps)
    ]
    for copy in weights_in + weights_down:
        copy.start()

    def unpack(group, carry):
        to = pl.ds(pl.multiple_of(group * GROUP_ROWS, GROUP_ROWS), GROUP_ROWS)
        unpack_group(swap_ref, 2, arrived_ref, group * group_block, rows_of, to)
        return carry

    lax.fori_loop(0, groups, unpack, 0, unroll=4)
    for step in range(steps):
        weights_in[step].wait()
        pieces = range(step * STEP_PIECES, (step + 1) * STEP_PIECES)
        rows = jnp.concatenate([rows_of[piece] for piece in pieces], 1)
        part = dot_f32(rows, in_ref[columns(step), :])
        if step == 0:
            gate_up[...] = part
        else:
            gate_up[...] += part
    active[...] = (jax.nn.silu(gate_up[:, :FF]) * gate_up[:, FF:]).astype(jnp.bfloat16)
    for step in range(steps):
        weights_down[step].wait()
        for piece in range(step * STEP_PIECES, (step + 1) * STEP_PIECES):
            rows_of[piece] = dot_f32(
                active[...], down_ref[:, piece * PIECE : (piece + 1) * PIECE]
            ).astype(jnp.bfloat16)

    def pack(group, carry):
        at = pl.ds(pl.multiple_of(group * GROUP_ROWS, GROUP_ROWS), GROUP_ROWS)
        second = (groups - 1 - group) * group_block + group_block // 2
        pack_group(swap_ref, rows_of, at, out_ref, group * group_block, second)
        return carry

    lax.fori_loop(0, groups, pack, 0, unroll=4)


def run_expert(arrived, swap, w_in, w_out):
    slots = arrived.shape[0] // PIECES
    any_spec = pl.BlockSpec(memory_space=pl.ANY)
    return pl.pallas_call(
        expert_kernel,
        out_shape=jax.ShapeDtypeStruct(arrived.shape, jnp.bfloat16),
        in_specs=[VMEM_SPEC, VMEM_SPEC, any_spec, any_spec],
        out_specs=VMEM_SPEC,
        scratch_shapes=[
            pltpu.VMEM(w_in.shape, jnp.bfloat16),
            pltpu.VMEM(w_out.shape, jnp.bfloat16),
            pltpu.SemaphoreType.DMA((2, PIECES // STEP_PIECES)),
            pltpu.VMEM((PIECES, slots, PIECE), jnp.bfloat16),
            pltpu.VMEM((slots, 2 * FF), jnp.float32),
            pltpu.VMEM((slots, FF), jnp.bfloat16),
        ],
        cost_estimate=pl.CostEstimate(
            flops=2 * slots * (w_in.size + w_out.size),
            bytes_accessed=2 * (2 * arrived.size + w_in.size + w_out.size),
            transcendentals=slots * FF,
        ),
        compiler_params=pltpu.CompilerParams(vmem_limit_bytes=EXPERT_VMEM),
        name="expert",
    )(arrived, swap, w_in, w_out)


def combine_kernel(target_ref, route_ref, hidden_ref, swap_ref, back_ref, out_ref, rows_of):
    step = pl.program_id(0)
    group_block = GROUP_ROWS * PIECES
    for part in range(STEP_GROUPS):
        to = (step * STEP_GROUPS + part) * GROUP_ROWS
        to = pl.ds(pl.multiple_of(to, GROUP_ROWS), GROUP_ROWS)
        unpack_group(swap_ref, 0, back_ref, part * group_block, rows_of, to)

    @pl.when(step == pl.num_programs(0) - 1)
    def _():
        slots, tokens = rows_of.shape[1], hidden_ref.shape[0]
        route = route_ref[...]
        mixing = route / jnp.sum(route, axis=-1, keepdims=True)
        slot = lax.broadcasted_iota(jnp.int32, (tokens, slots), 1)
        spread = jnp.zeros((tokens, slots), jnp.float32)
        for number in range(TOPK):
            spread += jnp.where(
                slot == target_ref[:, number : number + 1], mixing[:, number : number + 1], 0.0
            )
        high = spread.astype(jnp.bfloat16)
        low = (spread - high.astype(jnp.float32)).astype(jnp.bfloat16)
        both = jnp.concatenate([high, low], 0)
        for piece in range(PIECES):
            columns = slice(piece * PIECE, (piece + 1) * PIECE)
            mixed = dot_f32(both, rows_of[piece])
            out_ref[:, columns] = (
                hidden_ref[:, columns].astype(jnp.float32) + mixed[:tokens] + mixed[tokens:]
            ).astype(jnp.bfloat16)


def combine(target, route_weights, hidden, swap, back):
    tokens, model = hidden.shape
    slots = back.shape[0] // PIECES
    group_block = GROUP_ROWS * PIECES

    def whole(shape):
        return pl.BlockSpec(shape, lambda step: (0, 0))

    return pl.pallas_call(
        combine_kernel,
        grid=(slots // (GROUP_ROWS * STEP_GROUPS),),
        out_shape=jax.ShapeDtypeStruct((tokens, model), jnp.bfloat16),
        in_specs=[
            whole((tokens, TOPK)),
            whole((tokens, TOPK)),
            whole((tokens, model)),
            pl.BlockSpec(swap.shape, lambda step: (0, 0, 0)),
            pl.BlockSpec((STEP_GROUPS * group_block, PIECE), lambda step: (step, 0)),
        ],
        out_specs=whole((tokens, model)),
        scratch_shapes=[pltpu.VMEM((PIECES, slots, PIECE), jnp.bfloat16)],
        compiler_params=pltpu.CompilerParams(vmem_limit_bytes=VMEM_BYTES),
        name="combine",
    )(target, route_weights, hidden, swap, back)


def body(
    queries, keys, values, out_proj, residual, norm_gain, expert_ids, route_weights, w_in, w_out
):
    ctx_count = lax.axis_size("ctx")
    dev_count = ctx_count * lax.axis_size("tp")
    ctx_index = lax.axis_index("ctx")
    heads_here = queries.shape[1] // HEAD_DIM
    kv_index = lax.axis_index("tp") * heads_here // (HEADS // KV_HEADS)
    half = queries.shape[0] // 2

    flat_ids = expert_ids.reshape(-1)
    one_hot = (flat_ids[:, None] == jnp.arange(dev_count, dtype=jnp.int32)[None, :]).astype(
        jnp.int32
    )
    earlier = jnp.cumsum(one_hot, axis=0) - one_hot
    target = (flat_ids * CAP + jnp.sum(earlier * one_hot, axis=1)).reshape(expert_ids.shape)
    swap = piece_swap()

    opposite = [(i, ctx_count - 1 - i) for i in range(ctx_count)]
    swapped = lax.ppermute(queries[half:], "ctx", opposite)
    parity = lax.axis_index("tp") % 2
    place = jnp.stack(
        [2 * ctx_count - 1 - 2 * ctx_index, 2 * ctx_index, parity, kv_index]
    ).astype(jnp.int32)
    mine = lax.all_gather(own_half(place, keys, values, half), "ctx", axis=0, tiled=True)
    swapped, mine = lax.optimization_barrier((swapped, mine))
    other = lax.ppermute(mine, "tp", [(i, i ^ 1) for i in range(lax.axis_size("tp"))])
    full_proj = lax.all_gather(out_proj, "ctx", axis=0, tiled=False)
    projected = project(attend(place, swapped, queries[:half], mine, other), full_proj)
    attn_out = lax.psum_scatter(projected, "tp", scatter_dimension=0, tiled=True)

    tp_count = dev_count // ctx_count
    home = [
        (c * tp_count + t, (c if 2 * t < tp_count else ctx_count - 1 - c) * tp_count + t)
        for c in range(ctx_count)
        for t in range(tp_count)
    ]

    def trade(array):
        return lax.ppermute(array, ("ctx", "tp"), home)

    residual, projected = lax.optimization_barrier((residual, projected))
    hidden, packed = dispatch(
        trade(target).T, attn_out, trade(residual), norm_gain.reshape(1, -1), dev_count
    )

    def exchange(messages):
        shaped = messages.reshape(dev_count, CAP * PIECES, PIECE)
        arrived = lax.all_to_all(shaped, ("ctx", "tp"), split_axis=0, concat_axis=0, tiled=True)
        return arrived.reshape(dev_count * CAP * PIECES, PIECE)

    hidden, arrived = lax.optimization_barrier((hidden, exchange(packed)))
    processed = run_expert(arrived, swap, w_in[0], w_out[0])
    hidden, processed = lax.optimization_barrier((trade(hidden), processed))
    return combine(target, route_weights, hidden, swap, exchange(processed))


def solution(mesh):
    return jax.shard_map(
        body,
        mesh=mesh,
        in_specs=(
            P("ctx", "tp"),
            P("ctx", None),
            P("ctx", None),
            P("tp", "ctx"),
            P(("ctx", "tp"), None),
            P(),
            P(("ctx", "tp"), None),
            P(("ctx", "tp"), None),
            P(("ctx", "tp"), None, None),
            P(("ctx", "tp"), None, None),
        ),
        out_specs=P(("ctx", "tp"), None),
        check_vma=False,
    )
```

```python
import functools
import math

import jax
import jax.numpy as jnp
import numpy as np
from jax import lax
from jax.experimental import pallas as pl
from jax.experimental.pallas import tpu as pltpu
from jax.sharding import PartitionSpec as P

HEADS = 32
KV_HEADS = 2
HEAD_DIM = 128
FF = 768
TOPK = 4
CAP = 6
BASE2_SCALE = math.log2(math.e) / math.sqrt(HEAD_DIM)
EXPONENT_LIMIT = 100.0
KEY_WIDTH = 1024
SUB_ROWS = 512
WIDE_ROWS = 2048
PIECE = 512
PIECES = 8
GROUP = 8
GROUP_ROWS = GROUP * CAP
DISPATCH_GROUPS = 8
STEP_GROUPS = 4
STEP_PIECES = 2
PROJECT_WIDTH = 2048
VMEM_BYTES = 56 * 2**20
ATTEND_VMEM = 36 * 2**20

VMEM_SPEC = pl.BlockSpec(memory_space=pltpu.VMEM)
SMEM_SPEC = pl.BlockSpec(memory_space=pltpu.SMEM)


def piece_swap():
    devices = GROUP // 2
    length = PIECES * CAP
    swap = np.zeros((3, devices * length, devices * length), np.float32)
    for device in range(devices):
        for piece in range(PIECES):
            for slot in range(CAP):
                to = (piece * devices + device) * CAP + slot
                swap[0, to, device * length + piece * CAP + slot] = 1
                swap[2, to, device * length + tile_row(piece, slot)] = 1
    swap[1] = swap[0].T
    return jnp.asarray(swap, jnp.bfloat16)


def tile_row(piece, slot):
    if piece < CAP:
        return piece * 8 + slot
    return ((piece - CAP) * (CAP // 2) + slot // 2) * 8 + CAP + slot % 2


def unpack_group(swap_ref, which, message_ref, first, rows_of, to):
    size = swap_ref.shape[1]
    part = size // PIECES
    halves = [
        dot_f32(swap_ref[which], message_ref[pl.ds(pl.multiple_of(first + half * size, size), size), :])
        for half in range(2)
    ]
    for piece in range(PIECES):
        rows_of[piece, to, :] = jnp.concatenate(
            [half[piece * part : (piece + 1) * part] for half in halves], 0
        ).astype(jnp.bfloat16)


def pack_group(swap_ref, rows_of, at, message_ref, first):
    size = swap_ref.shape[1]
    part = size // PIECES
    pieces = [rows_of[piece, at, :].astype(jnp.float32) for piece in range(PIECES)]
    for half in range(2):
        stacked = jnp.concatenate([rows[half * part : (half + 1) * part] for rows in pieces], 0)
        to = first + half * size
        message_ref[pl.ds(pl.multiple_of(to, size), size), :] = dot_f32(
            swap_ref[1], stacked.astype(jnp.bfloat16)
        ).astype(jnp.bfloat16)


def dot_f32(left, right):
    return jnp.dot(left, right, preferred_element_type=jnp.float32)


def dot_keys(left, keys):
    return lax.dot_general(
        left, keys, (((1,), (1,)), ((), ())), preferred_element_type=jnp.float32
    )


def own_half_kernel(place_ref, keys_ref, values_ref, out_ref):
    out_ref[:, :HEAD_DIM] = keys_ref[...]
    out_ref[:, HEAD_DIM:] = values_ref[...]


def own_half(place, keys, values, half):
    taken = pl.BlockSpec((half, HEAD_DIM), lambda step, place_ref: (place_ref[2], place_ref[3]))
    return pl.pallas_call(
        own_half_kernel,
        grid_spec=pltpu.PrefetchScalarGridSpec(
            num_scalar_prefetch=1,
            grid=(1,),
            in_specs=[taken, taken],
            out_specs=pl.BlockSpec((half, 2 * HEAD_DIM), lambda step, place_ref: (0, 0)),
        ),
        out_shape=jax.ShapeDtypeStruct((half, 2 * HEAD_DIM), jnp.bfloat16),
        name="own_half",
    )(place, keys, values)


def attend_part(block, shift, parity, q_ref, mine_ref, other_ref, out_ref, q_wide, top, acc):
    rows, width, sub = q_ref.shape[0], KEY_WIDTH, SUB_ROWS
    heads = q_ref.shape[1] // HEAD_DIM
    tiles = heads * rows // sub
    last = (block * rows) // width
    bound = jnp.full((1, 1), jnp.inf, jnp.float32)
    ones = jnp.ones((acc.shape[0] - HEAD_DIM, width), jnp.bfloat16)

    def load(index, ordered=False):
        at = pl.ds(pl.multiple_of(index * (width // 2), width // 2), width // 2)
        first, second = mine_ref[at, :], other_ref[at, :]
        if ordered:
            swapped = parity > 0
            first, second = jnp.where(swapped, second, first), jnp.where(swapped, first, second)
        both = jnp.concatenate([first, second], 0)
        keys, values = both[:, :HEAD_DIM], both[:, HEAD_DIM:]
        return jnp.concatenate([keys, keys], 1), jnp.concatenate([values.T, ones], 0)

    norms = []
    for head in range(heads):
        scaled = q_ref[:, head * HEAD_DIM : (head + 1) * HEAD_DIM].astype(jnp.float32) * BASE2_SCALE
        high = scaled.astype(jnp.bfloat16)
        q_wide[head * rows : (head + 1) * rows, :HEAD_DIM] = high
        q_wide[head * rows : (head + 1) * rows, HEAD_DIM:] = (
            scaled - high.astype(jnp.float32)
        ).astype(jnp.bfloat16)
        norms.append(jnp.max(jnp.sum(scaled * scaled, axis=1, keepdims=True), axis=0, keepdims=True))
    longest_query = jnp.sqrt(functools.reduce(jnp.maximum, norms))

    keys, values = load(last, ordered=True)
    least = jnp.full((1, sub), jnp.inf, jnp.float32)
    for tile in range(tiles):
        at = slice(tile * sub, (tile + 1) * sub)
        first = (tile * sub) % rows
        seen = shift + first + sub
        scores = dot_keys(keys[:seen], q_wide[at, :])
        key = lax.broadcasted_iota(jnp.int32, (seen, sub), 0)
        row = lax.broadcasted_iota(jnp.int32, (seen, sub), 1) + (first + shift)
        scores = jnp.where(key <= row, scores, -1e30)
        best = jnp.max(scores, axis=0, keepdims=True)
        weights = jnp.exp2(scores - best).astype(jnp.bfloat16)
        acc[:, at] = dot_f32(values[:, :seen], weights)
        top[:, at] = jnp.broadcast_to(best, (top.shape[0], sub))
        least = jnp.minimum(least, best)
    bound = (EXPONENT_LIMIT + jnp.min(least, axis=1, keepdims=True)) / longest_query

    def longest(index, so_far):
        at = pl.ds(pl.multiple_of(index * (width // 2), width // 2), width // 2)
        for held in (mine_ref, other_ref):
            keys = held[at, :HEAD_DIM].astype(jnp.float32)
            length = jnp.sum(keys * keys, axis=1, keepdims=True)
            so_far = jnp.maximum(so_far, jnp.max(length, axis=0, keepdims=True))
        return so_far

    key_norm = jnp.sqrt(lax.fori_loop(0, last, longest, jnp.zeros((1, 1), jnp.float32)))
    safe = jnp.max(key_norm - bound) <= 0.0

    @pl.when(safe)
    def _():
        def step(index, carry):
            keys, values = load(index)
            for first in range(0, heads * rows, WIDE_ROWS):
                at = slice(first, first + WIDE_ROWS)
                scores = dot_keys(keys, q_wide[at, :])
                weights = jnp.exp2(scores - top[:1, at]).astype(jnp.bfloat16)
                acc[:, at] += dot_f32(values, weights)
            return carry

        lax.fori_loop(0, last, step, 0)

    @pl.when(jnp.logical_not(safe))
    def _():
        def step(index, carry):
            keys, values = load(index)
            for tile in range(tiles):
                at = slice(tile * sub, (tile + 1) * sub)
                scores = dot_keys(keys, q_wide[at, :])
                old = top[:1, at]
                best = jnp.maximum(old, jnp.max(scores, axis=0, keepdims=True))
                weights = jnp.exp2(scores - best).astype(jnp.bfloat16)
                acc[:, at] = acc[:, at] * jnp.exp2(old - best) + dot_f32(values, weights)
                top[:, at] = jnp.broadcast_to(best, (top.shape[0], sub))
            return carry

        lax.fori_loop(0, last, step, 0)

    for head in range(heads):
        at = slice(head * rows, (head + 1) * rows)
        mean = acc[:HEAD_DIM, at] / acc[HEAD_DIM : HEAD_DIM + 1, at]
        out_ref[:, head * HEAD_DIM : (head + 1) * HEAD_DIM] = mean.T.astype(jnp.bfloat16)


def attend_kernel(place_ref, far_ref, near_ref, mine_ref, other_ref, out_ref, *scratch):
    rows = near_ref.shape[0]
    near_out, far_out = out_ref.at[pl.ds(0, rows), :], out_ref.at[pl.ds(rows, rows), :]
    parity = place_ref[2]
    attend_part(place_ref[0], rows, parity, far_ref, mine_ref, other_ref, far_out, *scratch)
    attend_part(place_ref[1], 0, parity, near_ref, mine_ref, other_ref, near_out, *scratch)


def attend(place, far, near, mine, other):
    rows, columns = near.shape
    all_rows = rows * columns // HEAD_DIM
    return pl.pallas_call(
        attend_kernel,
        out_shape=jax.ShapeDtypeStruct((2 * rows, columns), jnp.bfloat16),
        in_specs=[SMEM_SPEC] + [VMEM_SPEC] * 4,
        out_specs=VMEM_SPEC,
        scratch_shapes=[
            pltpu.VMEM((all_rows, 2 * HEAD_DIM), jnp.bfloat16),
            pltpu.VMEM((8, all_rows), jnp.float32),
            pltpu.VMEM((HEAD_DIM + 16, all_rows), jnp.float32),
        ],
        compiler_params=pltpu.CompilerParams(vmem_limit_bytes=ATTEND_VMEM),
        name="attend",
    )(place, far, near, mine, other)


def project_kernel(attended_ref, proj_ref, out_ref):
    proj = jnp.concatenate([proj_ref[part] for part in range(proj_ref.shape[0])], 1)
    out_ref[...] = dot_f32(attended_ref[...], proj).astype(jnp.bfloat16)


def project(attended, proj):
    rows, depth = attended.shape
    parts, _, width = proj.shape
    taken = PROJECT_WIDTH // width
    return pl.pallas_call(
        project_kernel,
        grid=(parts // taken,),
        out_shape=jax.ShapeDtypeStruct((rows, parts * width), jnp.bfloat16),
        in_specs=[
            pl.BlockSpec((rows, depth), lambda step: (0, 0)),
            pl.BlockSpec((taken, depth, width), lambda step: (step, 0, 0)),
        ],
        out_specs=pl.BlockSpec((rows, taken * width), lambda step: (0, step)),
        compiler_params=pltpu.CompilerParams(vmem_limit_bytes=VMEM_BYTES),
        name="project",
    )(attended, proj)


def dispatch_kernel(target_ref, attn_ref, residual_ref, gain_ref, hidden_ref, out_ref, normed):
    step = pl.program_id(0)
    tokens = attn_ref.shape[0]
    devices = out_ref.shape[0]

    @pl.when(step == 0)
    def _():
        hidden = (
            residual_ref[...].astype(jnp.float32) + attn_ref[...].astype(jnp.float32)
        ).astype(jnp.bfloat16)
        hidden_ref[...] = hidden
        wide = hidden.astype(jnp.float32)
        variance = jnp.mean(wide * wide, axis=-1, keepdims=True)
        normed[...] = (wide * lax.rsqrt(variance + 1e-06) * gain_ref[...]).astype(jnp.bfloat16)

    number = lax.broadcasted_iota(jnp.int32, (devices * 8, tokens), 0)
    row = number & 7
    first = (step * devices + (number >> 3)) * CAP

    def chosen(slot):
        found = jnp.zeros(slot.shape, jnp.float32)
        for route in range(TOPK):
            found += jnp.where(slot == target_ref[route : route + 1, :], 1.0, 0.0)
        return found.astype(jnp.bfloat16)

    def columns(piece):
        return normed[:, piece * PIECE : (piece + 1) * PIECE]

    main = chosen(jnp.where(row < CAP, first + row, -1))
    tails = [
        chosen(jnp.where(row >= CAP, first + row - CAP + 2 * pair, -1)) for pair in range(CAP // 2)
    ]
    for pair in range(CAP // 2):
        tiles = []
        for tile in (2 * pair, 2 * pair + 1):
            taken = jnp.concatenate([main, tails[tile % (CAP // 2)]], 1)
            source = jnp.concatenate([columns(tile), columns(CAP + tile // (CAP // 2))], 0)
            tiles.append(dot_f32(taken, source).reshape(devices, 8, PIECE))
        out_ref[:, pair * 16 : (pair + 1) * 16, :] = jnp.concatenate(tiles, 1).astype(jnp.bfloat16)


def dispatch(target, attn_out, residual, gain, dev_count):
    tokens, model = residual.shape
    devices = GROUP * DISPATCH_GROUPS

    def whole(shape):
        return pl.BlockSpec(shape, lambda step: (0, 0))

    return pl.pallas_call(
        dispatch_kernel,
        grid=(dev_count // devices,),
        out_shape=(
            jax.ShapeDtypeStruct((tokens, model), jnp.bfloat16),
            jax.ShapeDtypeStruct((dev_count, CAP * PIECES, PIECE), jnp.bfloat16),
        ),
        in_specs=[
            whole((TOPK, tokens)),
            whole((tokens, model)),
            whole((tokens, model)),
            whole((1, model)),
        ],
        out_specs=(
            whole((tokens, model)),
            pl.BlockSpec((devices, CAP * PIECES, PIECE), lambda step: (step, 0, 0)),
        ),
        scratch_shapes=[pltpu.VMEM((tokens, model), jnp.bfloat16)],
        compiler_params=pltpu.CompilerParams(vmem_limit_bytes=VMEM_BYTES),
        name="norm_and_dispatch",
    )(target, attn_out, residual, gain)


def expert_kernel(
    arrived_hbm, swap_ref, in_hbm, down_hbm, out_hbm, in_ref, down_ref, landed, messages, moved, left, rows_of, gate_up, active
):
    group_block = GROUP_ROWS * PIECES
    groups = rows_of.shape[1] // GROUP_ROWS
    steps = PIECES // STEP_PIECES
    width = STEP_PIECES * PIECE
    chunk_rows = STEP_GROUPS * group_block
    chunks = messages.shape[0] // chunk_rows

    def span(index, size):
        return pl.ds(pl.multiple_of(index * size, size), size)

    def arriving(chunk):
        at = span(chunk, chunk_rows)
        return pltpu.make_async_copy(arrived_hbm.at[at, :], messages.at[at, :], moved.at[0, chunk])

    def leaving(chunk, half):
        half_rows = group_block // 2
        for part in range(STEP_GROUPS):
            group = chunk * STEP_GROUPS + part
            home = group if half == 0 else groups - 1 - group
            source = pl.ds(pl.multiple_of((2 * group + half) * half_rows, half_rows), half_rows)
            to = pl.ds(pl.multiple_of((2 * home + half) * half_rows, half_rows), half_rows)
            yield pltpu.make_async_copy(
                messages.at[source, :], out_hbm.at[to, :], left.at[half, group]
            )

    def weights_in(step):
        at = span(step, width)
        return pltpu.make_async_copy(in_hbm.at[at, :], in_ref.at[at, :], landed.at[0, step])

    def weights_down(step):
        at = span(step, width)
        return pltpu.make_async_copy(down_hbm.at[:, at], down_ref.at[step], landed.at[1, step])

    for chunk in range(chunks):
        arriving(chunk).start()

    def unpack(chunk, carry):
        arriving(chunk).wait()
        weights_in(chunk).start()
        for part in range(STEP_GROUPS):
            group = chunk * STEP_GROUPS + part
            unpack_group(swap_ref, 2, messages, group * group_block, rows_of, span(group, GROUP_ROWS))
        return carry

    def up(step, carry):
        weights_in(step).wait()
        weights_down(step).start()
        first = step * STEP_PIECES
        rows = jnp.concatenate([rows_of[first + part] for part in range(STEP_PIECES)], 1)
        gate_up[...] += dot_f32(rows, in_ref[span(step, width), :])
        return carry

    def down(step, carry):
        weights_down(step).wait()
        for part in range(STEP_PIECES):
            rows_of[step * STEP_PIECES + part] = dot_f32(
                active[...], down_ref[step, :, part * PIECE : (part + 1) * PIECE]
            ).astype(jnp.bfloat16)
        return carry

    def pack(chunk, carry):
        for part in range(STEP_GROUPS):
            group = chunk * STEP_GROUPS + part
            pack_group(swap_ref, rows_of, span(group, GROUP_ROWS), messages, group * group_block)
        for half in range(2):
            for copy in leaving(chunk, half):
                copy.start()
        return carry

    def leave(chunk, carry):
        for half in range(2):
            for copy in leaving(chunk, half):
                copy.wait()
        return carry

    lax.fori_loop(0, chunks, unpack, 0)
    gate_up[...] = jnp.zeros_like(gate_up)
    lax.fori_loop(0, steps, up, 0)
    active[...] = (jax.nn.silu(gate_up[:, :FF]) * gate_up[:, FF:]).astype(jnp.bfloat16)
    lax.fori_loop(0, steps, down, 0)
    lax.fori_loop(0, chunks, pack, 0)
    lax.fori_loop(0, chunks, leave, 0)


def run_expert(arrived, swap, w_in, w_out):
    slots = arrived.shape[0] // PIECES
    any_spec = pl.BlockSpec(memory_space=pl.ANY)
    return pl.pallas_call(
        expert_kernel,
        out_shape=jax.ShapeDtypeStruct(arrived.shape, jnp.bfloat16),
        in_specs=[any_spec, VMEM_SPEC, any_spec, any_spec],
        out_specs=any_spec,
        scratch_shapes=[
            pltpu.VMEM(w_in.shape, jnp.bfloat16),
            pltpu.VMEM((PIECES // STEP_PIECES, FF, STEP_PIECES * PIECE), jnp.bfloat16),
            pltpu.SemaphoreType.DMA((2, PIECES // STEP_PIECES)),
            pltpu.VMEM(arrived.shape, jnp.bfloat16),
            pltpu.SemaphoreType.DMA((1, slots // (GROUP_ROWS * STEP_GROUPS))),
            pltpu.SemaphoreType.DMA((2, slots // GROUP_ROWS)),
            pltpu.VMEM((PIECES, slots, PIECE), jnp.bfloat16),
            pltpu.VMEM((slots, 2 * FF), jnp.float32),
            pltpu.VMEM((slots, FF), jnp.bfloat16),
        ],
        cost_estimate=pl.CostEstimate(
            flops=2 * slots * (w_in.size + w_out.size),
            bytes_accessed=2 * (2 * arrived.size + w_in.size + w_out.size),
            transcendentals=slots * FF,
        ),
        compiler_params=pltpu.CompilerParams(vmem_limit_bytes=VMEM_BYTES),
        name="expert",
    )(arrived, swap, w_in, w_out)


def combine_kernel(target_ref, route_ref, hidden_ref, swap_ref, back_ref, out_ref, rows_of):
    step = pl.program_id(0)
    group_block = GROUP_ROWS * PIECES
    for part in range(STEP_GROUPS):
        to = (step * STEP_GROUPS + part) * GROUP_ROWS
        to = pl.ds(pl.multiple_of(to, GROUP_ROWS), GROUP_ROWS)
        unpack_group(swap_ref, 0, back_ref, part * group_block, rows_of, to)

    @pl.when(step == pl.num_programs(0) - 1)
    def _():
        slots, tokens = rows_of.shape[1], hidden_ref.shape[0]
        route = route_ref[...]
        mixing = route / jnp.sum(route, axis=-1, keepdims=True)
        slot = lax.broadcasted_iota(jnp.int32, (tokens, slots), 1)
        spread = jnp.zeros((tokens, slots), jnp.float32)
        for number in range(TOPK):
            spread += jnp.where(
                slot == target_ref[:, number : number + 1], mixing[:, number : number + 1], 0.0
            )
        high = spread.astype(jnp.bfloat16)
        low = (spread - high.astype(jnp.float32)).astype(jnp.bfloat16)
        both = jnp.concatenate([high, low], 0)
        for piece in range(PIECES):
            columns = slice(piece * PIECE, (piece + 1) * PIECE)
            mixed = dot_f32(both, rows_of[piece])
            out_ref[:, columns] = (
                hidden_ref[:, columns].astype(jnp.float32) + mixed[:tokens] + mixed[tokens:]
            ).astype(jnp.bfloat16)


def combine(target, route_weights, hidden, swap, back):
    tokens, model = hidden.shape
    slots = back.shape[0] // PIECES
    group_block = GROUP_ROWS * PIECES

    def whole(shape):
        return pl.BlockSpec(shape, lambda step: (0, 0))

    return pl.pallas_call(
        combine_kernel,
        grid=(slots // (GROUP_ROWS * STEP_GROUPS),),
        out_shape=jax.ShapeDtypeStruct((tokens, model), jnp.bfloat16),
        in_specs=[
            whole((tokens, TOPK)),
            whole((tokens, TOPK)),
            whole((tokens, model)),
            pl.BlockSpec(swap.shape, lambda step: (0, 0, 0)),
            pl.BlockSpec((STEP_GROUPS * group_block, PIECE), lambda step: (step, 0)),
        ],
        out_specs=whole((tokens, model)),
        scratch_shapes=[pltpu.VMEM((PIECES, slots, PIECE), jnp.bfloat16)],
        compiler_params=pltpu.CompilerParams(vmem_limit_bytes=VMEM_BYTES),
        name="combine",
    )(target, route_weights, hidden, swap, back)


def body(
    queries, keys, values, out_proj, residual, norm_gain, expert_ids, route_weights, w_in, w_out
):
    ctx_count = lax.axis_size("ctx")
    dev_count = ctx_count * lax.axis_size("tp")
    ctx_index = lax.axis_index("ctx")
    heads_here = queries.shape[1] // HEAD_DIM
    kv_index = lax.axis_index("tp") * heads_here // (HEADS // KV_HEADS)
    half = queries.shape[0] // 2

    flat_ids = expert_ids.reshape(-1)
    one_hot = (flat_ids[:, None] == jnp.arange(dev_count, dtype=jnp.int32)[None, :]).astype(
        jnp.int32
    )
    earlier = jnp.cumsum(one_hot, axis=0) - one_hot
    target = (flat_ids * CAP + jnp.sum(earlier * one_hot, axis=1)).reshape(expert_ids.shape)
    swap = piece_swap()

    opposite = [(i, ctx_count - 1 - i) for i in range(ctx_count)]
    swapped = lax.ppermute(queries[half:], "ctx", opposite)
    parity = lax.axis_index("tp") % 2
    place = jnp.stack(
        [2 * ctx_count - 1 - 2 * ctx_index, 2 * ctx_index, parity, kv_index]
    ).astype(jnp.int32)
    mine = lax.all_gather(own_half(place, keys, values, half), "ctx", axis=0, tiled=True)
    swapped, mine = lax.optimization_barrier((swapped, mine))
    other = lax.ppermute(mine, "tp", [(i, i ^ 1) for i in range(lax.axis_size("tp"))])
    full_proj = lax.all_gather(out_proj, "ctx", axis=0, tiled=False)
    projected = project(attend(place, swapped, queries[:half], mine, other), full_proj)
    attn_out = lax.psum_scatter(projected, "tp", scatter_dimension=0, tiled=True)

    tp_count = dev_count // ctx_count
    home = [
        (c * tp_count + t, (c if 2 * t < tp_count else ctx_count - 1 - c) * tp_count + t)
        for c in range(ctx_count)
        for t in range(tp_count)
    ]

    def trade(array):
        return lax.ppermute(array, ("ctx", "tp"), home)

    residual, projected = lax.optimization_barrier((residual, projected))
    hidden, packed = dispatch(
        trade(target).T, attn_out, trade(residual), norm_gain.reshape(1, -1), dev_count
    )

    def exchange(messages):
        shaped = messages.reshape(dev_count, CAP * PIECES, PIECE)
        arrived = lax.all_to_all(shaped, ("ctx", "tp"), split_axis=0, concat_axis=0, tiled=True)
        return arrived.reshape(dev_count * CAP * PIECES, PIECE)

    hidden, arrived = lax.optimization_barrier((hidden, exchange(packed)))
    processed = run_expert(arrived, swap, w_in[0], w_out[0])
    hidden, processed = lax.optimization_barrier((trade(hidden), processed))
    return combine(target, route_weights, hidden, swap, exchange(processed))


def solution(mesh):
    return jax.shard_map(
        body,
        mesh=mesh,
        in_specs=(
            P("ctx", "tp"),
            P("ctx", None),
            P("ctx", None),
            P("tp", "ctx"),
            P(("ctx", "tp"), None),
            P(),
            P(("ctx", "tp"), None),
            P(("ctx", "tp"), None),
            P(("ctx", "tp"), None, None),
            P(("ctx", "tp"), None, None),
        ),
        out_specs=P(("ctx", "tp"), None),
        check_vma=False,
    )
```

```python
import functools
import math

import jax
import jax.numpy as jnp
import numpy as np
from jax import lax
from jax.experimental import pallas as pl
from jax.experimental.pallas import tpu as pltpu
from jax.sharding import PartitionSpec as P

HEADS = 32
KV_HEADS = 2
HEAD_DIM = 128
FF = 768
TOPK = 4
CAP = 6
BASE2_SCALE = math.log2(math.e) / math.sqrt(HEAD_DIM)
EXPONENT_LIMIT = 100.0
KEY_WIDTH = 1024
SUB_ROWS = 512
WIDE_ROWS = 2048
PIECE = 512
PIECES = 8
GROUP = 8
GROUP_ROWS = GROUP * CAP
DISPATCH_GROUPS = 8
COMBINE_GROUPS = 8
STEP_GROUPS = 4
STEP_PIECES = 2
PROJECT_WIDTH = 2048
VMEM_BYTES = 56 * 2**20
ATTEND_VMEM = 36 * 2**20

VMEM_SPEC = pl.BlockSpec(memory_space=pltpu.VMEM)
SMEM_SPEC = pl.BlockSpec(memory_space=pltpu.SMEM)


def piece_swap():
    devices = GROUP // 2
    length = PIECES * CAP
    swap = np.zeros((3, devices * length, devices * length), np.float32)
    for device in range(devices):
        for piece in range(PIECES):
            for slot in range(CAP):
                to = (piece * devices + device) * CAP + slot
                swap[0, to, device * length + piece * CAP + slot] = 1
                swap[2, to, device * length + tile_row(piece, slot)] = 1
    swap[1] = swap[0].T
    return jnp.asarray(swap, jnp.bfloat16)


def tile_row(piece, slot):
    if piece < CAP:
        return piece * 8 + slot
    return ((piece - CAP) * (CAP // 2) + slot // 2) * 8 + CAP + slot % 2


def unpack_group(swap_ref, which, message_ref, first, rows_of, to):
    size = swap_ref.shape[1]
    part = size // PIECES
    halves = [
        dot_f32(swap_ref[which], message_ref[pl.ds(pl.multiple_of(first + half * size, size), size), :])
        for half in range(2)
    ]
    for piece in range(PIECES):
        rows_of[piece, to, :] = jnp.concatenate(
            [half[piece * part : (piece + 1) * part] for half in halves], 0
        ).astype(jnp.bfloat16)


def pack_group(swap_ref, rows_of, at, message_ref, first):
    size = swap_ref.shape[1]
    part = size // PIECES
    pieces = [rows_of[piece, at, :].astype(jnp.float32) for piece in range(PIECES)]
    for half in range(2):
        stacked = jnp.concatenate([rows[half * part : (half + 1) * part] for rows in pieces], 0)
        to = first + half * size
        message_ref[pl.ds(pl.multiple_of(to, size), size), :] = dot_f32(
            swap_ref[1], stacked.astype(jnp.bfloat16)
        ).astype(jnp.bfloat16)


def dot_f32(left, right):
    return jnp.dot(left, right, preferred_element_type=jnp.float32)


def dot_keys(left, keys):
    return lax.dot_general(
        left, keys, (((1,), (1,)), ((), ())), preferred_element_type=jnp.float32
    )


def own_half_kernel(place_ref, keys_ref, values_ref, out_ref):
    out_ref[:, :HEAD_DIM] = keys_ref[...]
    out_ref[:, HEAD_DIM:] = values_ref[...]


def own_half(place, keys, values, half):
    taken = pl.BlockSpec((half, HEAD_DIM), lambda step, place_ref: (place_ref[2], place_ref[3]))
    return pl.pallas_call(
        own_half_kernel,
        grid_spec=pltpu.PrefetchScalarGridSpec(
            num_scalar_prefetch=1,
            grid=(1,),
            in_specs=[taken, taken],
            out_specs=pl.BlockSpec((half, 2 * HEAD_DIM), lambda step, place_ref: (0, 0)),
        ),
        out_shape=jax.ShapeDtypeStruct((half, 2 * HEAD_DIM), jnp.bfloat16),
        name="own_half",
    )(place, keys, values)


def attend_part(block, shift, parity, q_ref, mine_ref, other_ref, out_ref, q_wide, top, acc):
    rows, width, sub = q_ref.shape[0], KEY_WIDTH, SUB_ROWS
    heads = q_ref.shape[1] // HEAD_DIM
    tiles = heads * rows // sub
    last = (block * rows) // width
    bound = jnp.full((1, 1), jnp.inf, jnp.float32)
    ones = jnp.ones((acc.shape[0] - HEAD_DIM, width), jnp.bfloat16)

    def load(index, ordered=False):
        at = pl.ds(pl.multiple_of(index * (width // 2), width // 2), width // 2)
        first, second = mine_ref[at, :], other_ref[at, :]
        if ordered:
            swapped = parity > 0
            first, second = jnp.where(swapped, second, first), jnp.where(swapped, first, second)
        both = jnp.concatenate([first, second], 0)
        keys, values = both[:, :HEAD_DIM], both[:, HEAD_DIM:]
        return jnp.concatenate([keys, keys], 1), jnp.concatenate([values.T, ones], 0)

    norms = []
    for head in range(heads):
        scaled = q_ref[:, head * HEAD_DIM : (head + 1) * HEAD_DIM].astype(jnp.float32) * BASE2_SCALE
        high = scaled.astype(jnp.bfloat16)
        q_wide[head * rows : (head + 1) * rows, :HEAD_DIM] = high
        q_wide[head * rows : (head + 1) * rows, HEAD_DIM:] = (
            scaled - high.astype(jnp.float32)
        ).astype(jnp.bfloat16)
        norms.append(jnp.max(jnp.sum(scaled * scaled, axis=1, keepdims=True), axis=0, keepdims=True))
    longest_query = jnp.sqrt(functools.reduce(jnp.maximum, norms))

    keys, values = load(last, ordered=True)
    least = jnp.full((1, sub), jnp.inf, jnp.float32)
    for tile in range(tiles):
        at = slice(tile * sub, (tile + 1) * sub)
        first = (tile * sub) % rows
        seen = shift + first + sub
        scores = dot_keys(keys[:seen], q_wide[at, :])
        key = lax.broadcasted_iota(jnp.int32, (seen, sub), 0)
        row = lax.broadcasted_iota(jnp.int32, (seen, sub), 1) + (first + shift)
        scores = jnp.where(key <= row, scores, -1e30)
        best = jnp.max(scores, axis=0, keepdims=True)
        weights = jnp.exp2(scores - best).astype(jnp.bfloat16)
        acc[:, at] = dot_f32(values[:, :seen], weights)
        top[:, at] = jnp.broadcast_to(best, (top.shape[0], sub))
        least = jnp.minimum(least, best)
    bound = (EXPONENT_LIMIT + jnp.min(least, axis=1, keepdims=True)) / longest_query

    def longest(index, so_far):
        at = pl.ds(pl.multiple_of(index * (width // 2), width // 2), width // 2)
        for held in (mine_ref, other_ref):
            keys = held[at, :HEAD_DIM].astype(jnp.float32)
            length = jnp.sum(keys * keys, axis=1, keepdims=True)
            so_far = jnp.maximum(so_far, jnp.max(length, axis=0, keepdims=True))
        return so_far

    key_norm = jnp.sqrt(lax.fori_loop(0, last, longest, jnp.zeros((1, 1), jnp.float32)))
    safe = jnp.max(key_norm - bound) <= 0.0

    @pl.when(safe)
    def _():
        def step(index, carry):
            keys, values = load(index)
            for first in range(0, heads * rows, WIDE_ROWS):
                at = slice(first, first + WIDE_ROWS)
                scores = dot_keys(keys, q_wide[at, :])
                weights = jnp.exp2(scores - top[:1, at]).astype(jnp.bfloat16)
                acc[:, at] += dot_f32(values, weights)
            return carry

        lax.fori_loop(0, last, step, 0)

    @pl.when(jnp.logical_not(safe))
    def _():
        def step(index, carry):
            keys, values = load(index)
            for tile in range(tiles):
                at = slice(tile * sub, (tile + 1) * sub)
                scores = dot_keys(keys, q_wide[at, :])
                old = top[:1, at]
                best = jnp.maximum(old, jnp.max(scores, axis=0, keepdims=True))
                weights = jnp.exp2(scores - best).astype(jnp.bfloat16)
                acc[:, at] = acc[:, at] * jnp.exp2(old - best) + dot_f32(values, weights)
                top[:, at] = jnp.broadcast_to(best, (top.shape[0], sub))
            return carry

        lax.fori_loop(0, last, step, 0)

    for head in range(heads):
        at = slice(head * rows, (head + 1) * rows)
        mean = acc[:HEAD_DIM, at] / acc[HEAD_DIM : HEAD_DIM + 1, at]
        out_ref[:, head * HEAD_DIM : (head + 1) * HEAD_DIM] = mean.T.astype(jnp.bfloat16)


def attend_kernel(place_ref, far_ref, near_ref, mine_ref, other_ref, out_ref, *scratch):
    rows = near_ref.shape[0]
    near_out, far_out = out_ref.at[pl.ds(0, rows), :], out_ref.at[pl.ds(rows, rows), :]
    parity = place_ref[2]
    attend_part(place_ref[0], rows, parity, far_ref, mine_ref, other_ref, far_out, *scratch)
    attend_part(place_ref[1], 0, parity, near_ref, mine_ref, other_ref, near_out, *scratch)


def attend(place, far, near, mine, other):
    rows, columns = near.shape
    all_rows = rows * columns // HEAD_DIM
    return pl.pallas_call(
        attend_kernel,
        out_shape=jax.ShapeDtypeStruct((2 * rows, columns), jnp.bfloat16),
        in_specs=[SMEM_SPEC] + [VMEM_SPEC] * 4,
        out_specs=VMEM_SPEC,
        scratch_shapes=[
            pltpu.VMEM((all_rows, 2 * HEAD_DIM), jnp.bfloat16),
            pltpu.VMEM((8, all_rows), jnp.float32),
            pltpu.VMEM((HEAD_DIM + 16, all_rows), jnp.float32),
        ],
        compiler_params=pltpu.CompilerParams(vmem_limit_bytes=ATTEND_VMEM),
        name="attend",
    )(place, far, near, mine, other)


def project_kernel(attended_ref, proj_ref, out_ref):
    proj = jnp.concatenate([proj_ref[part] for part in range(proj_ref.shape[0])], 1)
    out_ref[...] = dot_f32(attended_ref[...], proj).astype(jnp.bfloat16)


def project(attended, proj):
    rows, depth = attended.shape
    parts, _, width = proj.shape
    taken = PROJECT_WIDTH // width
    return pl.pallas_call(
        project_kernel,
        grid=(parts // taken,),
        out_shape=jax.ShapeDtypeStruct((rows, parts * width), jnp.bfloat16),
        in_specs=[
            pl.BlockSpec((rows, depth), lambda step: (0, 0)),
            pl.BlockSpec((taken, depth, width), lambda step: (step, 0, 0)),
        ],
        out_specs=pl.BlockSpec((rows, taken * width), lambda step: (0, step)),
        compiler_params=pltpu.CompilerParams(vmem_limit_bytes=VMEM_BYTES),
        name="project",
    )(attended, proj)


def dispatch_kernel(target_ref, attn_ref, residual_ref, gain_ref, hidden_ref, out_ref, normed):
    step = pl.program_id(0)
    tokens = attn_ref.shape[0]
    devices = out_ref.shape[0]

    @pl.when(step == 0)
    def _():
        hidden = (
            residual_ref[...].astype(jnp.float32) + attn_ref[...].astype(jnp.float32)
        ).astype(jnp.bfloat16)
        hidden_ref[...] = hidden
        wide = hidden.astype(jnp.float32)
        variance = jnp.mean(wide * wide, axis=-1, keepdims=True)
        normed[...] = (wide * lax.rsqrt(variance + 1e-06) * gain_ref[...]).astype(jnp.bfloat16)

    number = lax.broadcasted_iota(jnp.int32, (devices * 8, tokens), 0)
    row = number & 7
    first = (step * devices + (number >> 3)) * CAP

    def chosen(slot):
        found = jnp.zeros(slot.shape, jnp.float32)
        for route in range(TOPK):
            found += jnp.where(slot == target_ref[route : route + 1, :], 1.0, 0.0)
        return found.astype(jnp.bfloat16)

    def columns(piece):
        return normed[:, piece * PIECE : (piece + 1) * PIECE]

    main = chosen(jnp.where(row < CAP, first + row, -1))
    tails = [
        chosen(jnp.where(row >= CAP, first + row - CAP + 2 * pair, -1)) for pair in range(CAP // 2)
    ]
    for pair in range(CAP // 2):
        tiles = []
        for tile in (2 * pair, 2 * pair + 1):
            taken = jnp.concatenate([main, tails[tile % (CAP // 2)]], 1)
            source = jnp.concatenate([columns(tile), columns(CAP + tile // (CAP // 2))], 0)
            tiles.append(dot_f32(taken, source).reshape(devices, 8, PIECE))
        out_ref[:, pair * 16 : (pair + 1) * 16, :] = jnp.concatenate(tiles, 1).astype(jnp.bfloat16)


def dispatch(target, attn_out, residual, gain, dev_count):
    tokens, model = residual.shape
    devices = GROUP * DISPATCH_GROUPS

    def whole(shape):
        return pl.BlockSpec(shape, lambda step: (0, 0))

    return pl.pallas_call(
        dispatch_kernel,
        grid=(dev_count // devices,),
        out_shape=(
            jax.ShapeDtypeStruct((tokens, model), jnp.bfloat16),
            jax.ShapeDtypeStruct((dev_count, CAP * PIECES, PIECE), jnp.bfloat16),
        ),
        in_specs=[
            whole((TOPK, tokens)),
            whole((tokens, model)),
            whole((tokens, model)),
            whole((1, model)),
        ],
        out_specs=(
            whole((tokens, model)),
            pl.BlockSpec((devices, CAP * PIECES, PIECE), lambda step: (step, 0, 0)),
        ),
        scratch_shapes=[pltpu.VMEM((tokens, model), jnp.bfloat16)],
        compiler_params=pltpu.CompilerParams(vmem_limit_bytes=VMEM_BYTES),
        name="norm_and_dispatch",
    )(target, attn_out, residual, gain)


def expert_kernel(
    arrived_hbm, swap_ref, in_hbm, down_hbm, out_hbm, in_ref, down_ref, landed, messages, moved, left, rows_of, gate_up, active
):
    group_block = GROUP_ROWS * PIECES
    groups = rows_of.shape[1] // GROUP_ROWS
    steps = PIECES // STEP_PIECES
    width = STEP_PIECES * PIECE
    chunk_rows = STEP_GROUPS * group_block
    chunks = messages.shape[0] // chunk_rows

    def span(index, size):
        return pl.ds(pl.multiple_of(index * size, size), size)

    def arriving(chunk):
        at = span(chunk, chunk_rows)
        return pltpu.make_async_copy(arrived_hbm.at[at, :], messages.at[at, :], moved.at[0, chunk])

    def leaving(chunk, half):
        half_rows = group_block // 2
        for part in range(STEP_GROUPS):
            group = chunk * STEP_GROUPS + part
            home = group if half == 0 else groups - 1 - group
            source = pl.ds(pl.multiple_of((2 * group + half) * half_rows, half_rows), half_rows)
            to = pl.ds(pl.multiple_of((2 * home + half) * half_rows, half_rows), half_rows)
            yield pltpu.make_async_copy(
                messages.at[source, :], out_hbm.at[to, :], left.at[half, group]
            )

    def weights_in(step):
        at = span(step, width)
        return pltpu.make_async_copy(in_hbm.at[at, :], in_ref.at[at, :], landed.at[0, step])

    def weights_down(step):
        at = span(step, width)
        return pltpu.make_async_copy(down_hbm.at[:, at], down_ref.at[step], landed.at[1, step])

    for chunk in range(chunks):
        arriving(chunk).start()

    def unpack(chunk, carry):
        arriving(chunk).wait()
        weights_in(chunk).start()
        for part in range(STEP_GROUPS):
            group = chunk * STEP_GROUPS + part
            unpack_group(swap_ref, 2, messages, group * group_block, rows_of, span(group, GROUP_ROWS))
        return carry

    def up(step, carry):
        weights_in(step).wait()
        weights_down(step).start()
        first = step * STEP_PIECES
        rows = jnp.concatenate([rows_of[first + part] for part in range(STEP_PIECES)], 1)
        gate_up[...] += dot_f32(rows, in_ref[span(step, width), :])
        return carry

    def down(step, carry):
        weights_down(step).wait()
        for part in range(STEP_PIECES):
            rows_of[step * STEP_PIECES + part] = dot_f32(
                active[...], down_ref[step, :, part * PIECE : (part + 1) * PIECE]
            ).astype(jnp.bfloat16)
        return carry

    def pack(chunk, carry):
        for part in range(STEP_GROUPS):
            group = chunk * STEP_GROUPS + part
            pack_group(swap_ref, rows_of, span(group, GROUP_ROWS), messages, group * group_block)
        for half in range(2):
            for copy in leaving(chunk, half):
                copy.start()
        return carry

    def leave(chunk, carry):
        for half in range(2):
            for copy in leaving(chunk, half):
                copy.wait()
        return carry

    lax.fori_loop(0, chunks, unpack, 0)
    gate_up[...] = jnp.zeros_like(gate_up)
    lax.fori_loop(0, steps, up, 0)
    active[...] = (jax.nn.silu(gate_up[:, :FF]) * gate_up[:, FF:]).astype(jnp.bfloat16)
    lax.fori_loop(0, steps, down, 0)
    lax.fori_loop(0, chunks, pack, 0)
    lax.fori_loop(0, chunks, leave, 0)


def run_expert(arrived, swap, w_in, w_out):
    slots = arrived.shape[0] // PIECES
    any_spec = pl.BlockSpec(memory_space=pl.ANY)
    return pl.pallas_call(
        expert_kernel,
        out_shape=jax.ShapeDtypeStruct(arrived.shape, jnp.bfloat16),
        in_specs=[any_spec, VMEM_SPEC, any_spec, any_spec],
        out_specs=any_spec,
        scratch_shapes=[
            pltpu.VMEM(w_in.shape, jnp.bfloat16),
            pltpu.VMEM((PIECES // STEP_PIECES, FF, STEP_PIECES * PIECE), jnp.bfloat16),
            pltpu.SemaphoreType.DMA((2, PIECES // STEP_PIECES)),
            pltpu.VMEM(arrived.shape, jnp.bfloat16),
            pltpu.SemaphoreType.DMA((1, slots // (GROUP_ROWS * STEP_GROUPS))),
            pltpu.SemaphoreType.DMA((2, slots // GROUP_ROWS)),
            pltpu.VMEM((PIECES, slots, PIECE), jnp.bfloat16),
            pltpu.VMEM((slots, 2 * FF), jnp.float32),
            pltpu.VMEM((slots, FF), jnp.bfloat16),
        ],
        cost_estimate=pl.CostEstimate(
            flops=2 * slots * (w_in.size + w_out.size),
            bytes_accessed=2 * (2 * arrived.size + w_in.size + w_out.size),
            transcendentals=slots * FF,
        ),
        compiler_params=pltpu.CompilerParams(vmem_limit_bytes=VMEM_BYTES),
        name="expert",
    )(arrived, swap, w_in, w_out)


def combine_kernel(target_ref, route_ref, hidden_ref, swap_ref, back_ref, out_ref, rows_of):
    step = pl.program_id(0)
    group_block = GROUP_ROWS * PIECES
    for part in range(COMBINE_GROUPS):
        to = (step * COMBINE_GROUPS + part) * GROUP_ROWS
        to = pl.ds(pl.multiple_of(to, GROUP_ROWS), GROUP_ROWS)
        unpack_group(swap_ref, 0, back_ref, part * group_block, rows_of, to)

    @pl.when(step == pl.num_programs(0) - 1)
    def _():
        slots, tokens = rows_of.shape[1], hidden_ref.shape[0]
        route = route_ref[...]
        mixing = route / jnp.sum(route, axis=-1, keepdims=True)
        slot = lax.broadcasted_iota(jnp.int32, (tokens, slots), 1)
        spread = jnp.zeros((tokens, slots), jnp.float32)
        for number in range(TOPK):
            spread += jnp.where(
                slot == target_ref[:, number : number + 1], mixing[:, number : number + 1], 0.0
            )
        high = spread.astype(jnp.bfloat16)
        low = (spread - high.astype(jnp.float32)).astype(jnp.bfloat16)
        both = jnp.concatenate([high, low], 0)
        for piece in range(PIECES):
            columns = slice(piece * PIECE, (piece + 1) * PIECE)
            mixed = dot_f32(both, rows_of[piece])
            out_ref[:, columns] = (
                hidden_ref[:, columns].astype(jnp.float32) + mixed[:tokens] + mixed[tokens:]
            ).astype(jnp.bfloat16)


def combine(target, route_weights, hidden, swap, back):
    tokens, model = hidden.shape
    slots = back.shape[0] // PIECES
    group_block = GROUP_ROWS * PIECES

    def whole(shape):
        return pl.BlockSpec(shape, lambda step: (0, 0))

    return pl.pallas_call(
        combine_kernel,
        grid=(slots // (GROUP_ROWS * COMBINE_GROUPS),),
        out_shape=jax.ShapeDtypeStruct((tokens, model), jnp.bfloat16),
        in_specs=[
            whole((tokens, TOPK)),
            whole((tokens, TOPK)),
            whole((tokens, model)),
            pl.BlockSpec(swap.shape, lambda step: (0, 0, 0)),
            pl.BlockSpec((COMBINE_GROUPS * group_block, PIECE), lambda step: (step, 0)),
        ],
        out_specs=whole((tokens, model)),
        scratch_shapes=[pltpu.VMEM((PIECES, slots, PIECE), jnp.bfloat16)],
        compiler_params=pltpu.CompilerParams(vmem_limit_bytes=VMEM_BYTES),
        name="combine",
    )(target, route_weights, hidden, swap, back)


def body(
    queries, keys, values, out_proj, residual, norm_gain, expert_ids, route_weights, w_in, w_out
):
    ctx_count = lax.axis_size("ctx")
    dev_count = ctx_count * lax.axis_size("tp")
    ctx_index = lax.axis_index("ctx")
    heads_here = queries.shape[1] // HEAD_DIM
    kv_index = lax.axis_index("tp") * heads_here // (HEADS // KV_HEADS)
    half = queries.shape[0] // 2

    flat_ids = expert_ids.reshape(-1)
    one_hot = (flat_ids[:, None] == jnp.arange(dev_count, dtype=jnp.int32)[None, :]).astype(
        jnp.int32
    )
    earlier = jnp.cumsum(one_hot, axis=0) - one_hot
    target = (flat_ids * CAP + jnp.sum(earlier * one_hot, axis=1)).reshape(expert_ids.shape)
    swap = piece_swap()

    opposite = [(i, ctx_count - 1 - i) for i in range(ctx_count)]
    swapped = lax.ppermute(queries[half:], "ctx", opposite)
    parity = lax.axis_index("tp") % 2
    place = jnp.stack(
        [2 * ctx_count - 1 - 2 * ctx_index, 2 * ctx_index, parity, kv_index]
    ).astype(jnp.int32)
    mine = lax.all_gather(own_half(place, keys, values, half), "ctx", axis=0, tiled=True)
    swapped, mine = lax.optimization_barrier((swapped, mine))
    other = lax.ppermute(mine, "tp", [(i, i ^ 1) for i in range(lax.axis_size("tp"))])
    full_proj = lax.all_gather(out_proj, "ctx", axis=0, tiled=False)
    projected = project(attend(place, swapped, queries[:half], mine, other), full_proj)
    attn_out = lax.psum_scatter(projected, "tp", scatter_dimension=0, tiled=True)

    tp_count = dev_count // ctx_count
    home = [
        (c * tp_count + t, (c if 2 * t < tp_count else ctx_count - 1 - c) * tp_count + t)
        for c in range(ctx_count)
        for t in range(tp_count)
    ]

    def trade(array):
        return lax.ppermute(array, ("ctx", "tp"), home)

    residual, projected = lax.optimization_barrier((residual, projected))
    hidden, packed = dispatch(
        trade(target).T, attn_out, trade(residual), norm_gain.reshape(1, -1), dev_count
    )

    def exchange(messages):
        shaped = messages.reshape(dev_count, CAP * PIECES, PIECE)
        arrived = lax.all_to_all(shaped, ("ctx", "tp"), split_axis=0, concat_axis=0, tiled=True)
        return arrived.reshape(dev_count * CAP * PIECES, PIECE)

    hidden, arrived = lax.optimization_barrier((hidden, exchange(packed)))
    processed = run_expert(arrived, swap, w_in[0], w_out[0])
    hidden, processed = lax.optimization_barrier((trade(hidden), processed))
    return combine(target, route_weights, hidden, swap, exchange(processed))


def solution(mesh):
    return jax.shard_map(
        body,
        mesh=mesh,
        in_specs=(
            P("ctx", "tp"),
            P("ctx", None),
            P("ctx", None),
            P("tp", "ctx"),
            P(("ctx", "tp"), None),
            P(),
            P(("ctx", "tp"), None),
            P(("ctx", "tp"), None),
            P(("ctx", "tp"), None, None),
            P(("ctx", "tp"), None, None),
        ),
        out_specs=P(("ctx", "tp"), None),
        check_vma=False,
    )
```
